256 devices in a mesh: tile: 64 (over z_hi, x, y, core), head: 4 (over z_lo).
Axes of the slice: x: 4, y: 4, z: 8 (z_hi: 2, z_lo: 4; z = z_hi * 4 + z_lo), core: 2. Of those that a mesh axis runs over, the one named last changes fastest.
Arguments:
- queries: bfloat16 [65536, 1024], P('tile', 'head'), may hold values from -240 to 240
- keys: bfloat16 [65536, 1024], P('tile', 'head'), may hold values from -6 to 6, as said below
- values: bfloat16 [65536, 1024], P('tile', 'head'), may hold values from -6 to 6
- out_weight: bfloat16 [1024, 1024], replicated, may hold values from -0.1875 to 0.1875
- cotangent: bfloat16 [65536, 1024], P('tile', 'head'), may hold values from -6 to 6
Outputs:
- output: bfloat16 [65536, 1024], P('tile', 'head')
- grad_queries: bfloat16 [65536, 1024], P('tile', 'head')
- grad_keys: bfloat16 [65536, 1024], P('tile', 'head')
- grad_values: bfloat16 [65536, 1024], P('tile', 'head')
- weight_grad: float32 [1024, 1024], P('head')
The draws below stay inside these ranges and needn't reach their ends.
Inputs may be any that keep to these rules, and one draw needn't show every extreme that they name: keys of order one.
All inputs are finite; a program needn't handle non-finite values.
Results may differ from the reference program's by a relative error of at most 0.015.
Values may be sent and summed in bfloat16 or wider, within the bound.
A program may use at most 192 MiB of HBM per device.

```python
import math
import jax
import jax.numpy as jnp
from jax import lax

D = 1024
HEADS = 16
TILE = 256
POOLED = 64
TOK_DEV = 1024
TOKENS = 65536
N_TILE = 64


def shared_normal(key):
    return jnp.clip(jax.random.normal(key, (TOKENS, D), jnp.float32), -6.0, 6.0)


def draw_keys(key, part):
    base = shared_normal(key)
    return base.astype(jnp.bfloat16)


def draw_queries(key, part):
    key = jax.random.fold_in(key, 5)
    first = jax.random.fold_in(key, 0)
    fresh = jnp.clip(jax.random.normal(first, (TOKENS, D), jnp.float32), -6.0, 6.0)
    return fresh.astype(jnp.bfloat16)


def level_of(key, shape, cuts, low, largest):
    def one(axis_at, blocks):
        steps = jax.random.uniform(jax.random.fold_in(jax.random.fold_in(key, 6), axis_at), (blocks,), jnp.float32, low / len(cuts), largest / len(cuts))
        return jnp.repeat(jnp.exp(steps), shape[axis_at] // blocks).reshape((-1,) + (1,) * (len(shape) - axis_at - 1))

    loudness = one(*cuts[0])
    for cut in cuts[1:]:
        loudness = loudness * one(*cut)
    return loudness


def bell_draw(stream_key, dims, spread, most, cuts=(), held_as=jnp.bfloat16):
    values = jax.random.normal(stream_key, dims, jnp.float32) * spread
    if len(cuts) > 0:
        values = level_of(stream_key, dims, cuts, -0.22, 0.18) * values
    return jnp.clip(values, min=-most, max=most).astype(held_as)


def setup_inputs(seed: int = 0) -> dict:
    seeds = jax.random.split(jax.random.key(seed), 6)
    return {
        "queries": draw_queries(jax.random.fold_in(seeds[5], 71), 0),
        "keys": draw_keys(jax.random.fold_in(seeds[5], 71), 0),
        "values": bell_draw(seeds[2], (TOKENS, D), 1.0, 6.0, ((0, 64), (1, 4))),
        "out_weight": bell_draw(seeds[3], (D, D), D ** -0.5, 0.1875),
        "cotangent": bell_draw(seeds[4], (TOKENS, D), 1.0, 6.0, ((0, 64), (1, 4))),
    }


ROOT_HALF = 1.0 / math.sqrt(2.0)

def pool_nodes(nodes):
    count = nodes.shape[0]
    summed = nodes.astype(jnp.float32).reshape(count // 2, POOLED, 2, nodes.shape[2]).sum(2)
    return (summed * ROOT_HALF).astype(jnp.bfloat16)

def flip_pairs(nodes):
    count = nodes.shape[0]
    return nodes.reshape(count // 2, 2, POOLED, nodes.shape[2])[:, ::-1].reshape(count, POOLED, nodes.shape[2])

def spread_nodes(nodes):
    count = nodes.shape[0]
    return jnp.repeat(nodes * ROOT_HALF, 2, axis=1).reshape(2 * count, POOLED, nodes.shape[2])

def summarize(tokens, count, group):
    total = tokens.astype(jnp.float32).reshape(count * POOLED, group, tokens.shape[1]).sum(1)
    return (total * (1.0 / math.sqrt(group))).astype(jnp.bfloat16).reshape(count, POOLED, tokens.shape[1])

def round_barrier(array):
    lowered = lax.optimization_barrier(array.astype(jnp.bfloat16))
    return lowered.astype(jnp.float32)

def probabilities(query_blocks, key_all, scale):
    scores = jnp.einsum('tqhd,tkhd->thqk', query_blocks, key_all) * scale
    top_score = lax.optimization_barrier(jnp.max(scores, axis=-1, keepdims=True))
    weights = jnp.exp(scores - top_score)
    return weights / lax.optimization_barrier(jnp.sum(weights, axis=-1, keepdims=True))

def reference(queries, keys, values, out_weight, cotangent):
    per_head = D // HEADS
    count = TOKENS // TILE
    tiles = TOK_DEV // TILE
    group = TILE // POOLED
    levels = count.bit_length() - 1
    scale = 1.0 / math.sqrt(per_head)
    node_k = summarize(keys, count, group)
    node_v = summarize(values, count, group)
    far_k = []
    far_v = []
    for level_no in range(levels):
        far_k.append(jnp.repeat(flip_pairs(node_k), 2 ** level_no, axis=0))
        far_v.append(jnp.repeat(flip_pairs(node_v), 2 ** level_no, axis=0))
        if level_no + 1 < levels:
            node_k = pool_nodes(node_k)
            node_v = pool_nodes(node_v)
    far_k = jnp.concatenate(far_k, axis=1)
    far_v = jnp.concatenate(far_v, axis=1)

    def blocks(array):
        return array.reshape(N_TILE, tiles, -1, array.shape[-1])

    def assemble(near, far):
        return jnp.concatenate([near, far], axis=1).astype(jnp.float32).reshape(tiles, -1, HEADS, per_head)

    def forward_block(inputs):
        query_in, key_in, value_in, key_far, value_far = inputs
        key_all = assemble(key_in, key_far)
        value_all = assemble(value_in, value_far)
        query_blocks = query_in.astype(jnp.float32).reshape(tiles, TILE, HEADS, per_head)
        probs = probabilities(query_blocks, key_all, scale)
        probs_low = round_barrier(probs)
        mixed_block = jnp.einsum('thqk,tkhd->tqhd', probs_low, value_all)
        return mixed_block.astype(jnp.bfloat16).reshape(tiles, TILE, D)
    parts = (blocks(queries), blocks(keys), blocks(values), blocks(far_k), blocks(far_v))
    mixed = lax.map(forward_block, parts).reshape(TOKENS, D)
    output = jnp.dot(mixed, out_weight, preferred_element_type=jnp.float32).astype(jnp.bfloat16)
    grad_mixed = jnp.dot(cotangent, out_weight.T, preferred_element_type=jnp.float32).astype(jnp.bfloat16)
    weight_grad = jnp.dot(mixed.T, cotangent, preferred_element_type=jnp.float32)

    def backward_block(inputs):
        query_in, key_in, value_in, key_far, value_far, grad_in = inputs
        key_all = assemble(key_in, key_far)
        value_all = assemble(value_in, value_far)
        query_blocks = query_in.astype(jnp.float32).reshape(tiles, TILE, HEADS, per_head)
        probs = probabilities(query_blocks, key_all, scale)
        probs_low = round_barrier(probs)
        grad_blocks = grad_in.astype(jnp.float32).reshape(tiles, TILE, HEADS, per_head)
        grad_probs = jnp.einsum('tqhd,tkhd->thqk', grad_blocks, value_all)
        centre = lax.optimization_barrier(jnp.sum(probs * grad_probs, axis=-1, keepdims=True))
        dscore = round_barrier(probs * (grad_probs - centre) * scale)
        grad_query = jnp.einsum('thqk,tkhd->tqhd', dscore, key_all).astype(jnp.bfloat16).reshape(tiles, TILE, D)
        grad_key = jnp.einsum('thqk,tqhd->tkhd', dscore, query_blocks).reshape(tiles, -1, D)
        grad_value = jnp.einsum('thqk,tqhd->tkhd', probs_low, grad_blocks).reshape(tiles, -1, D)
        return (grad_query, grad_key, grad_value)
    grad_query, grad_key, grad_value = lax.map(backward_block, parts + (blocks(grad_mixed),))
    grad_key = grad_key.reshape(count, -1, D)
    grad_value = grad_value.reshape(count, -1, D)

    def descend(far_grad):
        down_nodes = None
        for level_no in reversed(range(levels)):
            part_sum = far_grad[:, level_no].reshape(count >> level_no, 2 ** level_no, POOLED, D).sum(1)
            part_sum = flip_pairs(part_sum)
            if down_nodes is None:
                down_nodes = part_sum
            else:
                down_nodes = part_sum + spread_nodes(down_nodes)
        return jnp.repeat(down_nodes.reshape(count * POOLED, D) * (1.0 / math.sqrt(group)), group, axis=0)
    far_key = grad_key[:, TILE:].reshape(count, levels, POOLED, D)
    far_value = grad_value[:, TILE:].reshape(count, levels, POOLED, D)
    grad_keys = (grad_key[:, :TILE].reshape(TOKENS, D) + descend(far_key)).astype(jnp.bfloat16)
    grad_values = (grad_value[:, :TILE].reshape(TOKENS, D) + descend(far_value)).astype(jnp.bfloat16)
    return (output, grad_query.reshape(TOKENS, D), grad_keys, grad_values, weight_grad)
```

```python
import math

import jax
import jax.numpy as jnp
from jax import lax
from jax.experimental import pallas as pl
from jax.experimental.pallas import tpu as pltpu
from jax.sharding import PartitionSpec as P

BF = jnp.bfloat16
F32 = jnp.float32
MESH = pl.DeviceIdType.MESH
ROOT_HALF = 1.0 / math.sqrt(2.0)
NT = (((1,), (1,)), ((), ()))
TILE = 256
W = 256


def mm(a, b):
    return jnp.dot(a, b, preferred_element_type=F32)


def mm_nt(a, b):
    return lax.dot_general(a, b, NT, preferred_element_type=F32)


def iota(shape, axis):
    return lax.broadcasted_iota(jnp.int32, shape, axis)


def ones_where(mask):
    return jnp.where(mask, 1.0, 0.0).astype(BF)


def pool2(x):
    n = x.shape[0]
    pairs = ones_where((iota((n // 2, n), 1) >> 1) == iota((n // 2, n), 0))
    return (mm(pairs, x) * ROOT_HALF).astype(BF)


def repeat_rows(x, times_log2):
    n = x.shape[0]
    big = n << times_log2
    spread = ones_where((iota((big, n), 0) >> times_log2) == iota((big, n), 1))
    high = x.astype(BF)
    low = (x - high.astype(F32)).astype(BF)
    return mm(spread, high) + mm(spread, low)


def spread2(x):
    return repeat_rows(x, 1) * ROOT_HALF


def lanes(a, b):
    return jnp.concatenate([a, b], axis=1)


def stack_kv(x):
    return jnp.concatenate([x[:, :W], x[:, W:]], axis=0)


def unstack_kv(x):
    n = x.shape[0] // 2
    return jnp.concatenate([x[:n], x[n:]], axis=1)


def kernel(
    q_hbm, k_hbm, v_hbm, w_hbm, c_hbm,
    out_hbm, gq_hbm, gk_hbm, gv_hbm, wg_hbm,
    q_v, ks, vs, kst, vst, w_v, cot, pt_v, dst_v, mixt, mixf, mixed, ma, ob, outr, gq_v, gk_v, gv_v,
    qbd, gbd, dko, dvo, p0, p1, fg, wpart, ws, wr, ws2, wr2, wg3, wg4, wgo,
    u0, u1, u2, ru0, ru1, ru2, n3f, h0, h1, h2, rh0, rh1, rh2, fk, fv,
    e0, e1, e2, e3, e4, e5, re0, re1, re2, re3, re4, re5, d3s, rd3,
    in_sem, out_sem, ag_send, ag_recv, up_send, up_recv, uh_send, uh_recv,
    ma_send, ma_recv, ob_send, ob_recv,
    w1_send, w1_recv, w2_send, w2_recv, w3_send, w3_recv, w4_send, w4_recv,
    dl_send, dl_recv, dh_send, dh_recv, d3_send, d3_recv,
):
    pos = lax.axis_index("tile")
    h = lax.axis_index("head")
    i = pos & 7
    g = pos >> 3

    in_cot = [pltpu.make_async_copy(c_hbm.at[c], cot.at[h, c], in_sem.at[c]) for c in range(4)]
    in_k = [pltpu.make_async_copy(k_hbm.at[t], ks.at[t, pl.ds(0, TILE)], in_sem.at[4 + t]) for t in range(4)]
    in_v = [pltpu.make_async_copy(v_hbm.at[t], vs.at[t, pl.ds(0, TILE)], in_sem.at[8 + t]) for t in range(4)]
    in_q = pltpu.make_async_copy(q_hbm, q_v, in_sem.at[12])
    in_w = pltpu.make_async_copy(w_hbm, w_v, in_sem.at[13])
    for copy in in_k + in_v + in_cot + [in_q, in_w]:
        copy.start()

    barrier = pltpu.get_barrier_semaphore()
    for m in range(1, 8):
        pl.semaphore_signal(barrier, inc=1, device_id=(pos ^ m, h), device_id_type=MESH)
        pl.semaphore_signal(barrier, inc=1, device_id=(pos ^ (8 * m), h), device_id_type=MESH)
    for m in range(1, 4):
        pl.semaphore_signal(barrier, inc=1, device_id=(pos, h ^ m), device_id_type=MESH)
    pl.semaphore_wait(barrier, 17)

    def remote(src, dst, send_sem, recv_sem, to_pos, to_head):
        return pltpu.make_async_remote_copy(
            src_ref=src, dst_ref=dst, send_sem=send_sem, recv_sem=recv_sem,
            device_id=(to_pos, to_head), device_id_type=MESH,
        )

    def ag_right(k, c):
        return remote(cot.at[h - k, c], cot.at[h - k, c], ag_send.at[0, k, c], ag_recv.at[0, k, c], pos, h + 1)

    def ag_left(k, c):
        return remote(cot.at[h + k, c], cot.at[h + k, c], ag_send.at[1, k, c], ag_recv.at[1, k, c], pos, h - 1)

    def ag_wait_right(k, c):
        remote(cot.at[h - k, c], cot.at[h - k, c], ag_send.at[0, k - 1, c], ag_recv.at[0, k - 1, c], pos, h).wait_recv()

    def ag_wait_left(k, c):
        remote(cot.at[h + k, c], cot.at[h + k, c], ag_send.at[1, k - 1, c], ag_recv.at[1, k - 1, c], pos, h).wait_recv()

    def ag_forward(k, c):
        @pl.when(h - k >= 0)
        def _():
            ag_wait_right(k, c)

            @pl.when(h < 3)
            def _():
                ag_right(k, c).start()

        @pl.when(h + k <= 3)
        def _():
            ag_wait_left(k, c)

            @pl.when(h > 0)
            def _():
                ag_left(k, c).start()

    for copy in in_k + in_v:
        copy.wait()
    quads = ones_where((iota((64, TILE), 1) >> 2) == iota((64, TILE), 0))
    leaf = [
        (mm(quads, lanes(ks[t, 0:TILE, :], vs[t, 0:TILE, :])) * 0.5).astype(BF) for t in range(4)
    ]
    node1 = [pool2(jnp.concatenate([leaf[2 * n], leaf[2 * n + 1]], axis=0)) for n in range(2)]
    top = pool2(jnp.concatenate(node1, axis=0))
    pool_1 = pool2(top)
    pool_2 = pool2(pool_1)
    n = 16
    pairs = ones_where((iota((n // 2, n), 1) >> 1) == iota((n // 2, n), 0))
    pool_3f = (mm(pairs, pool_2) * ROOT_HALF).astype(BF).astype(F32)
    pool_3 = jnp.concatenate([pool_3f[:, :W], pool_3f[:, W:]], axis=0).astype(BF)
    u0[0:128, :] = stack_kv(top)
    u0[128:144, :] = pool_3
    u1[0:64, :] = stack_kv(pool_1)
    u1[64:80, :] = pool_3
    u2[0:32, :] = stack_kv(pool_2)
    u2[32:48, :] = pool_3

    def low_pair(m, s0, r0, s1, r1, s2, r2):
        if m == 1:
            return s0, r0
        if m < 4:
            return s1, r1.at[m - 2]
        return s2, r2.at[m - 4]

    up = []
    for m in range(1, 8):
        src, dst = low_pair(m, u0, ru0, u1, ru1, u2, ru2)
        up.append(remote(src, dst, up_send.at[m - 1], up_recv.at[m - 1], pos ^ m, h))
        up[-1].start()

    for copy in in_cot:
        copy.wait()
    for c in range(4):
        @pl.when(h < 3)
        def _():
            ag_right(0, c).start()

        @pl.when(h > 0)
        def _():
            ag_left(0, c).start()

    for t in range(4):
        other = leaf[t ^ 1]
        ks[t, 256:320, :] = other[:, :W]
        vs[t, 256:320, :] = other[:, W:]
        other = node1[(t >> 1) ^ 1]
        ks[t, 320:384, :] = other[:, :W]
        vs[t, 320:384, :] = other[:, W:]
        kst[t, :, 0:384] = ks[t, 0:384, :].T
        vst[t, :, 0:384] = vs[t, 0:384, :].T

    in_q.wait()
    in_w.wait()

    n3f[pl.ds(pl.multiple_of(i * 8, 8), 8), :] = jnp.concatenate([pool_3f[:, :W], pool_3f[:, W:]], axis=1)

    def put_group_part(part, sender):
        part = part.astype(F32)
        n3f[pl.ds(pl.multiple_of(sender * 8, 8), 8), :] = jnp.concatenate([part[0:8], part[8:16]], axis=1)

    for m in range(1, 8):
        up[m - 1].wait_recv()
        sender = i ^ m
        if m == 1:
            fk[0:64, :] = ru0[0:64, :]
            fv[0:64, :] = ru0[64:128, :]
            put_group_part(ru0[128:144, :], sender)
        elif m < 4:
            at = pl.multiple_of(64 + (sender & 1) * 32, 32)
            fk[pl.ds(at, 32), :] = ru1[m - 2, 0:32, :]
            fv[pl.ds(at, 32), :] = ru1[m - 2, 32:64, :]
            put_group_part(ru1[m - 2, 64:80, :], sender)
        else:
            at = pl.multiple_of(128 + (sender & 3) * 16, 16)
            fk[pl.ds(at, 16), :] = ru2[m - 4, 0:16, :]
            fv[pl.ds(at, 16), :] = ru2[m - 4, 16:32, :]
            put_group_part(ru2[m - 4, 32:48, :], sender)
    group_node = n3f[...].astype(BF)
    group_1 = pool2(group_node)
    group_2 = pool2(group_1)
    h0[...] = stack_kv(group_node)
    h1[...] = stack_kv(group_1)
    h2[...] = stack_kv(group_2)
    uh = []
    for m in range(1, 8):
        src, dst = low_pair(m, h0, rh0, h1, rh1, h2, rh2)
        uh.append(remote(src, dst, uh_send.at[m - 1], uh_recv.at[m - 1], pos ^ (8 * m), h))
        uh[-1].start()

    for c in range(4):
        ag_forward(1, c)

    for m in range(1, 8):
        uh[m - 1].wait_recv()
        sender = g ^ m
        if m == 1:
            fk[192:256, :] = rh0[0:64, :]
            fv[192:256, :] = rh0[64:128, :]
        elif m < 4:
            at = pl.multiple_of(256 + (sender & 1) * 32, 32)
            fk[pl.ds(at, 32), :] = rh1[m - 2, 0:32, :]
            fv[pl.ds(at, 32), :] = rh1[m - 2, 32:64, :]
        else:
            at = pl.multiple_of(320 + (sender & 3) * 16, 16)
            fk[pl.ds(at, 16), :] = rh2[m - 4, 0:16, :]
            fv[pl.ds(at, 16), :] = rh2[m - 4, 16:32, :]
    far_kt = fk[...].T
    far_vt = fv[...].T
    for t in range(4):
        ks[t, 384:768, :] = fk[...]
        vs[t, 384:768, :] = fv[...]
        kst[t, :, 384:768] = far_kt
        vst[t, :, 384:768] = far_vt

    head_masks = [ones_where((iota((TILE, W), 1) >> 6) == hd) for hd in range(4)]

    def forward(step, carry):
        t = (step + h + 1) & 3
        q_tile = q_v[t] * jnp.asarray(0.125, BF)
        for hd in range(4):
            scores = mm_nt(ks[t], q_tile * head_masks[hd])
            peak = jnp.max(scores, axis=0, keepdims=True)
            weights = jnp.exp(scores - peak)
            total = jnp.sum(weights, axis=0, keepdims=True)
            probs = (weights * (1.0 / total)).astype(BF)
            pt_v[t, :, hd * 256:(hd + 1) * 256] = probs
            mixf[t, hd * 64:(hd + 1) * 64, :] = mm(vst[t, hd * 64:(hd + 1) * 64, :], probs)
        whole = mixf[t]
        mixt[t] = whole.astype(BF)
        mixed[t] = whole.T.astype(BF)

        @pl.when(t != h)
        def _():
            remote(mixed.at[t], ma.at[h], ma_send.at[t], ma_recv.at[h], pos, t).start()

        @pl.when(t == h)
        def _():
            ma[h] = mixed[t]

        @pl.when(step >= 2)
        def _():
            ag_forward(2, 2 * step - 4)
            ag_forward(2, 2 * step - 3)

        return carry

    lax.fori_loop(0, 4, forward, 0)

    w1 = [
        remote(ws.at[i ^ m], wr.at[m], w1_send.at[m - 1], w1_recv.at[m - 1], pos ^ m, h)
        for m in range(1, 8)
    ]
    own_rows = pl.ds(pl.multiple_of(h * W, W), W)
    wpart[...] = jnp.zeros_like(wpart)
    fg[...] = jnp.zeros_like(fg)

    def backward(t, carry):
        @pl.when(h == 3)
        def _():
            ag_wait_right(3, t)

        @pl.when(h == 0)
        def _():
            ag_wait_left(3, t)

        gmt = mm_nt(w_v[own_rows, 0:W], cot[0, t])
        for s in range(1, 4):
            gmt = gmt + mm_nt(w_v[own_rows, s * W:(s + 1) * W], cot[s, t])
        for s in range(4):
            wpart[:, s * W:(s + 1) * W] += mm(mixt[t], cot[s, t])

        @pl.when(t == 3)
        def _():
            for r in range(8):
                ws[r] = wpart[r * 32:(r + 1) * 32, :].astype(BF)
            for copy in w1:
                copy.start()

        gm = gmt.T.astype(BF)
        gmt = gmt.astype(BF).astype(F32)
        q_tile = q_v[t] * jnp.asarray(0.125, BF)
        dqt = []
        for hd in range(4):
            at = slice(hd * 64, (hd + 1) * 64)
            block = slice(hd * 256, (hd + 1) * 256)
            gm_head = gm * head_masks[hd]
            gbd[block, :] = gm_head
            qbd[block, :] = q_tile * head_masks[hd]
            centre = jnp.sum(gmt[at] * mixf[t, at, :], axis=0, keepdims=True)
            grad_probs = mm_nt(vs[t], gm_head)
            dscore = (pt_v[t, :, block].astype(F32) * (grad_probs - centre)).astype(BF)
            dst_v[:, block] = dscore
            dqt.append(mm(kst[t, at, :], dscore))
        gq_v[t] = (jnp.concatenate(dqt, axis=0) * 0.125).T.astype(BF)
        pltpu.make_async_copy(gq_v.at[t], gq_hbm.at[t], out_sem.at[t]).start()
        dk = mm(dst_v[...], qbd[...])
        dv = mm(pt_v[t], gbd[...])
        dko[t] = dk[0:256]
        dvo[t] = dv[0:256]
        p0[t] = lanes(dk[256:320], dv[256:320])
        p1[t] = lanes(dk[320:384], dv[320:384])
        fg[...] += lanes(dk[384:768], dv[384:768])
        return carry

    lax.fori_loop(0, 4, backward, 0)

    def level(b):
        return fg[b * 64:(b + 1) * 64, :]

    def cut(buffer, b, parts):
        rows = 64 // parts
        whole = level(b)
        for part in range(parts):
            buffer[part] = stack_kv(whole[part * rows:(part + 1) * rows]).astype(BF)

    e3[...] = stack_kv(level(3)).astype(BF)
    cut(e4, 4, 2)
    cut(e5, 5, 4)

    def down_pair(m, index, s0, r0, s1, r1, s2, r2):
        if m == 1:
            return s0, r0
        if m < 4:
            return s1.at[(index ^ m) & 1], r1.at[m - 2]
        return s2.at[(index ^ m) & 3], r2.at[m - 4]

    dh = []
    for m in range(1, 8):
        src, dst = down_pair(m, g, e3, re3, e4, re4, e5, re5)
        dh.append(remote(src, dst, dh_send.at[m - 1], dh_recv.at[m - 1], pos ^ (8 * m), h))
        dh[-1].start()
    e0[...] = stack_kv(level(0)).astype(BF)
    cut(e1, 1, 2)
    cut(e2, 2, 4)
    dl = []
    for m in range(1, 8):
        src, dst = down_pair(m, i, e0, re0, e1, re1, e2, re2)
        dl.append(remote(src, dst, dl_send.at[m - 1], dl_recv.at[m - 1], pos ^ m, h))
        dl[-1].start()

    for copy in w1:
        copy.wait_recv()
    total = wpart[pl.ds(pl.multiple_of(i * 32, 32), 32), :]
    for m in range(1, 8):
        total = total + wr[m].astype(F32)
    for r in range(8):
        ws2[r] = total[:, r * 128:(r + 1) * 128].astype(BF)
    w2 = []
    for m in range(1, 8):
        w2.append(remote(ws2.at[g ^ m], wr2.at[m], w2_send.at[m - 1], w2_recv.at[m - 1], pos ^ (8 * m), h))
        w2[-1].start()

    for m in range(1, 4):
        remote(ma.at[h ^ m], ma.at[h ^ m], ma_send.at[h ^ m], ma_recv.at[h ^ m], pos, h).wait_recv()
    to_heads = []
    for c in range(4):
        block = mm(ma[0], w_v[0:W, c * W:(c + 1) * W])
        for s in range(1, 4):
            block = block + mm(ma[s], w_v[s * W:(s + 1) * W, c * W:(c + 1) * W])
        ob[c] = block.astype(BF)
    for m in range(1, 4):
        to_heads.append(
            remote(ob.at[h ^ m], outr.at[m], ob_send.at[m - 1], ob_recv.at[m - 1], pos, h ^ m)
        )
        to_heads[-1].start()
    own_out = pltpu.make_async_copy(ob.at[h], out_hbm.at[h], out_sem.at[4])
    own_out.start()

    for copy in dh:
        copy.wait_recv()

    def f32_kv(x):
        return unstack_kv(x.astype(F32))

    quarter = f32_kv(re5[0]) + f32_kv(re5[1]) + f32_kv(re5[2]) + f32_kv(re5[3])
    half = f32_kv(re4[0]) + f32_kv(re4[1]) + spread2(quarter)
    group_grad = f32_kv(re3[...]) + spread2(half)
    for r in range(8):
        d3s[r] = stack_kv(group_grad[r * 8:(r + 1) * 8]).astype(BF)
    d3 = []
    for m in range(1, 8):
        d3.append(remote(d3s.at[i ^ m], rd3.at[m], d3_send.at[m - 1], d3_recv.at[m - 1], pos ^ m, h))
        d3[-1].start()

    for copy in w2:
        copy.wait_recv()
    block = ws2[g].astype(F32)
    for m in range(1, 8):
        block = block + wr2[m].astype(F32)
    wg3[g] = block.astype(BF)
    w3 = []
    for m in range(1, 8):
        w3.append(remote(wg3.at[g], wg3.at[g], w3_send.at[m - 1], w3_recv.at[m - 1], pos ^ (8 * m), h))
        w3[-1].start()

    for copy in dl:
        copy.wait_recv()
    for copy in d3:
        copy.wait_recv()
    eighth = f32_kv(d3s[i])
    for m in range(1, 8):
        eighth = eighth + f32_kv(rd3[m])
    quarter = f32_kv(re2[0]) + f32_kv(re2[1]) + f32_kv(re2[2]) + f32_kv(re2[3]) + spread2(eighth)
    half = f32_kv(re1[0]) + f32_kv(re1[1]) + spread2(quarter)
    top_grad = f32_kv(re0[...]) + spread2(half)
    spread_top = spread2(top_grad)
    for n in range(2):
        first = 2 * (1 - n)
        down_1 = p1[first] + p1[first + 1] + spread_top[n * 64:(n + 1) * 64]
        spread_1 = spread2(down_1)
        for r in range(2):
            t = 2 * n + r
            down_0 = p0[t ^ 1] + spread_1[r * 64:(r + 1) * 64]
            back = repeat_rows(down_0, 2) * 0.5
            gk_v[t] = (dko[t] + back[:, :W]).astype(BF)
            gv_v[t] = (dvo[t] + back[:, W:]).astype(BF)
    out_k = pltpu.make_async_copy(gk_v, gk_hbm, out_sem.at[5])
    out_v = pltpu.make_async_copy(gv_v, gv_hbm, out_sem.at[6])
    out_k.start()
    out_v.start()

    for m in range(1, 8):
        remote(wg3.at[g ^ m], wg3.at[g ^ m], w3_send.at[m - 1], w3_recv.at[m - 1], pos, h).wait_recv()
    w4 = []
    for m in range(1, 8):
        w4.append(remote(wg3, wg4.at[m], w4_send.at[m - 1], w4_recv.at[m - 1], pos ^ m, h))
        w4[-1].start()

    out_parts = []
    for m in range(1, 4):
        to_heads[m - 1].wait_recv()
        out_parts.append(pltpu.make_async_copy(outr.at[m], out_hbm.at[h ^ m], out_sem.at[6 + m]))
        out_parts[-1].start()

    def put_rows(owner, blocks):
        rows = pl.ds(pl.multiple_of(owner * 32, 32), 32)
        for r in range(8):
            wgo[rows, r * 128:(r + 1) * 128] = blocks[r].astype(F32)

    put_rows(i, wg3[...])
    for m in range(1, 8):
        w4[m - 1].wait_recv()
        put_rows(i ^ m, wg4[m])
    out_w = pltpu.make_async_copy(wgo, wg_hbm, out_sem.at[10])
    out_w.start()

    for copy in up + uh + w1 + w2 + w3 + w4 + dl + dh + d3 + to_heads:
        copy.wait_send()
    for m in range(1, 4):
        t = h ^ m
        remote(mixed.at[t], ma.at[h], ma_send.at[t], ma_recv.at[h], pos, t).wait_send()
    for k in range(3):
        for c in range(4):
            @pl.when(jnp.logical_and(h - k >= 0, h < 3))
            def _():
                ag_right(k, c).wait_send()

            @pl.when(jnp.logical_and(h + k <= 3, h > 0))
            def _():
                ag_left(k, c).wait_send()
    for t in range(4):
        pltpu.make_async_copy(gq_v.at[t], gq_hbm.at[t], out_sem.at[t]).wait()
    for copy in [own_out, out_k, out_v, out_w] + out_parts:
        copy.wait()


def local(queries, keys, values, out_weight, cotangent):
    tiles = (4, TILE, W)
    any_space = pl.BlockSpec(memory_space=pl.ANY)

    def v(*shape, dtype=BF):
        return pltpu.VMEM(shape, dtype)

    def f(*shape):
        return pltpu.VMEM(shape, F32)

    dma = pltpu.SemaphoreType.DMA
    scratch = [
        v(4, 256, 256), v(4, 768, 256), v(4, 768, 256), v(4, 256, 768), v(4, 256, 768),
        v(1024, 1024), v(4, 4, 256, 256), v(4, 768, 1024), v(768, 1024),
        v(4, 256, 256), f(4, 256, 256), v(4, 256, 256), v(4, 256, 256),
        v(4, 256, 256), v(4, 256, 256), v(4, 256, 256), v(4, 256, 256), v(4, 256, 256),
        v(1024, 256), v(1024, 256), f(4, 256, 256), f(4, 256, 256),
        f(4, 64, 512), f(4, 64, 512), f(384, 512), f(256, 1024),
        v(8, 32, 1024), v(8, 32, 1024), v(8, 32, 128), v(8, 32, 128),
        v(8, 32, 128), v(8, 8, 32, 128), f(256, 1024),
        v(144, 256), v(80, 256), v(48, 256), v(144, 256), v(2, 80, 256), v(4, 48, 256),
        f(64, 512), v(128, 256), v(64, 256), v(32, 256),
        v(128, 256), v(2, 64, 256), v(4, 32, 256), v(384, 256), v(384, 256),
        v(128, 256), v(2, 64, 256), v(4, 32, 256), v(128, 256), v(2, 64, 256), v(4, 32, 256),
        v(128, 256), v(2, 64, 256), v(4, 32, 256), v(128, 256), v(2, 64, 256), v(4, 32, 256),
        v(8, 16, 256), v(8, 16, 256),
        dma((14,)), dma((11,)), dma((2, 3, 4)), dma((2, 3, 4)),
        dma((7,)), dma((7,)), dma((7,)), dma((7,)),
        dma((4,)), dma((4,)), dma((3,)), dma((3,)),
    ] + [dma((7,))] * 8 + [dma((7,))] * 6
    out_shape = [jax.ShapeDtypeStruct(tiles, BF)] * 4 + [jax.ShapeDtypeStruct((256, 1024), F32)]
    output, gq, gk, gv, wg = pl.pallas_call(
        kernel,
        out_shape=out_shape,
        in_specs=[any_space] * 5,
        out_specs=[any_space] * 5,
        scratch_shapes=scratch,
        compiler_params=pltpu.CompilerParams(
            collective_id=0, has_side_effects=True, vmem_limit_bytes=60 * 1024 * 1024
        ),
    )(
        queries.reshape(tiles), keys.reshape(tiles), values.reshape(tiles), out_weight,
        cotangent.reshape(tiles),
    )
    rows = queries.shape
    return output.reshape(rows), gq.reshape(rows), gk.reshape(rows), gv.reshape(rows), wg


def solution(mesh):
    in_specs = (P("tile", "head"), P("tile", "head"), P("tile", "head"), P(), P("tile", "head"))
    out_specs = (
        P("tile", "head"),
        P("tile", "head"),
        P("tile", "head"),
        P("tile", "head"),
        P("head", None),
    )
    return jax.shard_map(local, mesh=mesh, in_specs=in_specs, out_specs=out_specs, check_vma=False)
```

```python
import math

import jax
import jax.numpy as jnp
from jax import lax
from jax.experimental import pallas as pl
from jax.experimental.pallas import tpu as pltpu
from jax.sharding import PartitionSpec as P

BF = jnp.bfloat16
F32 = jnp.float32
MESH = pl.DeviceIdType.MESH
ROOT_HALF = 1.0 / math.sqrt(2.0)
NT = (((1,), (1,)), ((), ()))
TILE = 256
W = 256


def mm(a, b):
    return jnp.dot(a, b, preferred_element_type=F32)


def mm_nt(a, b):
    return lax.dot_general(a, b, NT, preferred_element_type=F32)


def iota(shape, axis):
    return lax.broadcasted_iota(jnp.int32, shape, axis)


def ones_where(mask):
    return jnp.where(mask, 1.0, 0.0).astype(BF)


def pool2(x):
    n = x.shape[0]
    pairs = ones_where((iota((n // 2, n), 1) >> 1) == iota((n // 2, n), 0))
    return (mm(pairs, x) * ROOT_HALF).astype(BF)


def repeat_rows(x, times_log2):
    n = x.shape[0]
    big = n << times_log2
    spread = ones_where((iota((big, n), 0) >> times_log2) == iota((big, n), 1))
    high = x.astype(BF)
    low = (x - high.astype(F32)).astype(BF)
    return mm(spread, high) + mm(spread, low)


def spread2(x):
    return repeat_rows(x, 1) * ROOT_HALF


def lanes(a, b):
    return jnp.concatenate([a, b], axis=1)


def stack_kv(x):
    return jnp.concatenate([x[:, :W], x[:, W:]], axis=0)


def unstack_kv(x):
    n = x.shape[0] // 2
    return jnp.concatenate([x[:n], x[n:]], axis=1)


def kernel(
    q_hbm, k_hbm, v_hbm, w_hbm, c_hbm,
    outr, gq_v, gk_v, gv_v, wgo,
    q_v, ks, vs, kst, vst, w_v, cot, pt_v, dst_v, mixt, mixf, mixed, ma, ob,
    qbd, gbd, dko, dvo, p0, p1, fg, wpart, wsa, wra, ws2a, wr2a, wg3a, wg4a,
    wsb, wrb, ws2b, wr2b, wg3b, wg4b,
    u0, u1, u2, ru0, ru1, ru2, n3f, h0, h1, h2, rh0, rh1, rh2, fk, fv,
    e0, e1, e2, e3, e4, e5, re0, re1, re2, re3, re4, re5, d3s, rd3,
    in_sem, ag_send, ag_recv, up_send, up_recv, uh_send, uh_recv,
    ma_send, ma_recv, ob_send, ob_recv,
    w1_send, w1_recv, w2_send, w2_recv, w3_send, w3_recv, w4_send, w4_recv,
    dl_send, dl_recv, dh_send, dh_recv, d3_send, d3_recv,
):
    pos = lax.axis_index("tile")
    h = lax.axis_index("head")
    i = pos & 7
    g = pos >> 3

    in_cot = [pltpu.make_async_copy(c_hbm.at[c], cot.at[h, c], in_sem.at[c]) for c in range(4)]
    in_k = [pltpu.make_async_copy(k_hbm.at[t], ks.at[t, pl.ds(0, TILE)], in_sem.at[4 + t]) for t in range(4)]
    in_v = [pltpu.make_async_copy(v_hbm.at[t], vs.at[t, pl.ds(0, TILE)], in_sem.at[8 + t]) for t in range(4)]
    in_q = pltpu.make_async_copy(q_hbm, q_v, in_sem.at[12])
    in_w = pltpu.make_async_copy(w_hbm, w_v, in_sem.at[13])
    for copy in in_k + in_v + in_cot + [in_q, in_w]:
        copy.start()

    barrier = pltpu.get_barrier_semaphore()
    for m in (4, 5, 6, 7, 2, 3, 1):
        pl.semaphore_signal(barrier, inc=1, device_id=(pos ^ (8 * m), h), device_id_type=MESH)
    for m in range(1, 4):
        pl.semaphore_signal(barrier, inc=1, device_id=(pos, h ^ m), device_id_type=MESH)
    for m in range(1, 8):
        pl.semaphore_signal(barrier, inc=1, device_id=(pos ^ m, h), device_id_type=MESH)

    def remote(src, dst, send_sem, recv_sem, to_pos, to_head):
        return pltpu.make_async_remote_copy(
            src_ref=src, dst_ref=dst, send_sem=send_sem, recv_sem=recv_sem,
            device_id=(to_pos, to_head), device_id_type=MESH,
        )

    def ag_right(k, c):
        return remote(cot.at[h - k, c], cot.at[h - k, c], ag_send.at[0, k, c], ag_recv.at[0, k, c], pos, h + 1)

    def ag_left(k, c):
        return remote(cot.at[h + k, c], cot.at[h + k, c], ag_send.at[1, k, c], ag_recv.at[1, k, c], pos, h - 1)

    def ag_wait_right(k, c):
        remote(cot.at[h - k, c], cot.at[h - k, c], ag_send.at[0, k - 1, c], ag_recv.at[0, k - 1, c], pos, h).wait_recv()

    def ag_wait_left(k, c):
        remote(cot.at[h + k, c], cot.at[h + k, c], ag_send.at[1, k - 1, c], ag_recv.at[1, k - 1, c], pos, h).wait_recv()

    def ag_forward(k, c):
        @pl.when(h - k >= 0)
        def _():
            ag_wait_right(k, c)

            @pl.when(h < 3)
            def _():
                ag_right(k, c).start()

        @pl.when(h + k <= 3)
        def _():
            ag_wait_left(k, c)

            @pl.when(h > 0)
            def _():
                ag_left(k, c).start()

    for copy in in_k + in_v:
        copy.wait()
    quads = ones_where((iota((64, TILE), 1) >> 2) == iota((64, TILE), 0))
    leaf = [
        (mm(quads, lanes(ks[t, 0:TILE, :], vs[t, 0:TILE, :])) * 0.5).astype(BF) for t in range(4)
    ]
    node1 = [pool2(jnp.concatenate([leaf[2 * n], leaf[2 * n + 1]], axis=0)) for n in range(2)]
    top = pool2(jnp.concatenate(node1, axis=0))
    pool_1 = pool2(top)
    pool_2 = pool2(pool_1)
    n = 16
    pairs = ones_where((iota((n // 2, n), 1) >> 1) == iota((n // 2, n), 0))
    pool_3f = (mm(pairs, pool_2) * ROOT_HALF).astype(BF).astype(F32)
    pool_3 = jnp.concatenate([pool_3f[:, :W], pool_3f[:, W:]], axis=0).astype(BF)
    u0[0:128, :] = stack_kv(top)
    u0[128:144, :] = pool_3
    u1[0:64, :] = stack_kv(pool_1)
    u1[64:80, :] = pool_3
    u2[0:32, :] = stack_kv(pool_2)
    u2[32:48, :] = pool_3

    for copy in in_cot:
        copy.wait()
    pl.semaphore_wait(barrier, 17)

    def low_pair(m, s0, r0, s1, r1, s2, r2):
        if m == 1:
            return s0, r0
        if m < 4:
            return s1, r1.at[m - 2]
        return s2, r2.at[m - 4]

    up = []
    for m in range(1, 8):
        src, dst = low_pair(m, u0, ru0, u1, ru1, u2, ru2)
        up.append(remote(src, dst, up_send.at[m - 1], up_recv.at[m - 1], pos ^ m, h))
        up[-1].start()

    for c in range(4):
        @pl.when(h < 3)
        def _():
            ag_right(0, c).start()

        @pl.when(h > 0)
        def _():
            ag_left(0, c).start()

    for t in range(4):
        other = leaf[t ^ 1]
        ks[t, 256:320, :] = other[:, :W]
        vs[t, 256:320, :] = other[:, W:]
        other = node1[(t >> 1) ^ 1]
        ks[t, 320:384, :] = other[:, :W]
        vs[t, 320:384, :] = other[:, W:]
        kst[t, :, 0:384] = ks[t, 0:384, :].T
        vst[t, :, 0:384] = vs[t, 0:384, :].T

    in_q.wait()
    in_w.wait()

    n3f[pl.ds(pl.multiple_of(i * 8, 8), 8), :] = jnp.concatenate([pool_3f[:, :W], pool_3f[:, W:]], axis=1)

    def put_group_part(part, sender):
        part = part.astype(F32)
        n3f[pl.ds(pl.multiple_of(sender * 8, 8), 8), :] = jnp.concatenate([part[0:8], part[8:16]], axis=1)

    for m in range(1, 8):
        up[m - 1].wait_recv()
        sender = i ^ m
        if m == 1:
            fk[0:64, :] = ru0[0:64, :]
            fv[0:64, :] = ru0[64:128, :]
            put_group_part(ru0[128:144, :], sender)
        elif m < 4:
            at = pl.multiple_of(64 + (sender & 1) * 32, 32)
            fk[pl.ds(at, 32), :] = ru1[m - 2, 0:32, :]
            fv[pl.ds(at, 32), :] = ru1[m - 2, 32:64, :]
            put_group_part(ru1[m - 2, 64:80, :], sender)
        else:
            at = pl.multiple_of(128 + (sender & 3) * 16, 16)
            fk[pl.ds(at, 16), :] = ru2[m - 4, 0:16, :]
            fv[pl.ds(at, 16), :] = ru2[m - 4, 16:32, :]
            put_group_part(ru2[m - 4, 32:48, :], sender)
    group_node = n3f[...].astype(BF)
    group_1 = pool2(group_node)
    group_2 = pool2(group_1)
    h0[...] = stack_kv(group_node)
    h1[...] = stack_kv(group_1)
    h2[...] = stack_kv(group_2)
    uh = []
    for m in range(1, 8):
        src, dst = low_pair(m, h0, rh0, h1, rh1, h2, rh2)
        uh.append(remote(src, dst, uh_send.at[m - 1], uh_recv.at[m - 1], pos ^ (8 * m), h))
        uh[-1].start()

    for c in range(4):
        ag_forward(1, c)

    for m in range(1, 8):
        uh[m - 1].wait_recv()
        sender = g ^ m
        if m == 1:
            fk[192:256, :] = rh0[0:64, :]
            fv[192:256, :] = rh0[64:128, :]
        elif m < 4:
            at = pl.multiple_of(256 + (sender & 1) * 32, 32)
            fk[pl.ds(at, 32), :] = rh1[m - 2, 0:32, :]
            fv[pl.ds(at, 32), :] = rh1[m - 2, 32:64, :]
        else:
            at = pl.multiple_of(320 + (sender & 3) * 16, 16)
            fk[pl.ds(at, 16), :] = rh2[m - 4, 0:16, :]
            fv[pl.ds(at, 16), :] = rh2[m - 4, 16:32, :]
    far_kt = fk[...].T
    far_vt = fv[...].T
    for t in range(4):
        ks[t, 384:768, :] = fk[...]
        vs[t, 384:768, :] = fv[...]
        kst[t, :, 384:768] = far_kt
        vst[t, :, 384:768] = far_vt

    head_masks = [ones_where((iota((TILE, W), 1) >> 6) == hd) for hd in range(4)]

    def send_mixed(t):
        return remote(
            mixed.at[t], ma.at[t & 1, h], ma_send.at[t], ma_recv.at[t & 1, h], pos, 1 + (t >> 1)
        )

    middle = jnp.logical_and(h > 0, h < 3)

    def forward(step, carry):
        t = (step + 2 * (1 - (h >> 1))) & 3
        q_tile = q_v[t] * jnp.asarray(0.125, BF)
        for hd in range(4):
            scores = mm_nt(ks[t], q_tile * head_masks[hd])
            peak = jnp.max(scores, axis=0, keepdims=True)
            weights = jnp.exp(scores - peak)
            total = jnp.sum(weights, axis=0, keepdims=True)
            probs = (weights * (1.0 / total)).astype(BF)
            pt_v[t, :, hd * 256:(hd + 1) * 256] = probs
            mixf[t, hd * 64:(hd + 1) * 64, :] = mm(vst[t, hd * 64:(hd + 1) * 64, :], probs)
        whole = mixf[t]
        mixt[t] = whole.astype(BF)
        mixed[t] = whole.T.astype(BF)

        owner = 1 + (t >> 1)

        @pl.when(h != owner)
        def _():
            send_mixed(t).start()

        @pl.when(h == owner)
        def _():
            ma[t & 1, h] = mixed[t]

        ag_forward(2, step)
        return carry

    lax.fori_loop(0, 4, forward, 0)

    upper = h >> 1
    order_a = (h, h ^ 1, 2 - upper)
    order_b = (3 * (1 - upper),)

    class Reduction:
        def __init__(self, order, part, bufs):
            self.order, self.part, self.nb = order, part, len(order)
            self.ws, self.wr, self.ws2, self.wr2, self.wg3, self.wg4 = bufs
            self.first = 0 if part == 0 else 3

        def begin(self):
            for j, s in enumerate(self.order):
                block = mm(mixt[0], cot[s, 0])
                for t in range(1, 4):
                    block = block + mm(mixt[t], cot[s, t])
                wpart[self.first + j] = block
                for r in range(8):
                    self.ws[r, :, j * W:(j + 1) * W] = block[r * 32:(r + 1) * 32].astype(BF)
            for copy in self.low():
                copy.start()

        def low(self):
            return [
                remote(self.ws.at[i ^ m], self.wr.at[m], w1_send.at[self.part, m - 1], w1_recv.at[self.part, m - 1], pos ^ m, h)
                for m in range(1, 8)
            ]

        def high(self):
            return [
                remote(self.ws2.at[(g ^ m) & 3], self.wr2.at[g], w2_send.at[self.part, m - 1], w2_recv.at[self.part, m - 1],
                       pos ^ (8 * m), h)
                for m in range(1, 8)
            ]

        def back_x(self):
            return [
                remote(self.wg3.at[g & 3], self.wg3.at[g & 3], w3_send.at[self.part, m - 1], w3_recv.at[self.part, m - 1],
                       pos ^ (8 * m), h)
                for m in range(1, 4)
            ]

        def back_low(self):
            return [
                remote(self.wg3, self.wg4.at[m], w4_send.at[self.part, m - 1], w4_recv.at[self.part, m - 1], pos ^ m, h)
                for m in range(1, 8)
            ]

        def to_high(self):
            for copy in self.low():
                copy.wait_recv()
            half = self.nb * 128
            rows = pl.ds(pl.multiple_of(i * 32, 32), 32)
            total = jnp.concatenate([wpart[self.first + j, rows, :] for j in range(self.nb)], axis=1)
            for m in range(1, 8):
                total = total + self.wr[m].astype(F32)
            for r in range(4):
                piece = total[r * 8:(r + 1) * 8]
                self.ws2[r] = jnp.concatenate([piece[:, :half], piece[:, half:]], axis=0).astype(BF)
            for copy in self.high():
                copy.start()
            self.wr2[g] = self.ws2[g & 3]

        def to_back_x(self):
            for m in range(1, 8):
                remote(self.ws2.at[0], self.wr2.at[g ^ m], w2_send.at[self.part, m - 1], w2_recv.at[self.part, m - 1], pos, h).wait_recv()
            total = self.wr2[0].astype(F32)
            for r in range(1, 8):
                total = total + self.wr2[r].astype(F32)
            self.wg3[g & 3] = total.astype(BF)
            for copy in self.back_x():
                copy.start()

        def to_back_low(self):
            for m in range(1, 4):
                slot = self.wg3.at[(g ^ m) & 3]
                remote(slot, slot, w3_send.at[self.part, m - 1], w3_recv.at[self.part, m - 1], pos, h).wait_recv()
            for copy in self.back_low():
                copy.start()
            self.wg4[0] = self.wg3[...]

        def finish(self):
            for copy in self.back_low():
                copy.wait_recv()
            half = self.nb * 128

            def put(m, carry):
                for r in range(4):
                    rows = pl.ds(pl.multiple_of((i ^ m) * 32 + r * 8, 8), 8)
                    piece = self.wg4[m, r].astype(F32)
                    for c in range(2 * self.nb):
                        top, lane = (c * 128) // half, (c * 128) % half
                        columns = pl.ds(pl.multiple_of(self.order[c // 2] * W + (c % 2) * 128, 128), 128)
                        wgo[rows, columns] = piece[top * 8:(top + 1) * 8, lane:lane + 128]
                return carry

            lax.fori_loop(0, 8, put, 0)

        def wait_sends(self):
            for copy in self.low() + self.high() + self.back_x() + self.back_low():
                copy.wait_send()

    part_a = Reduction(order_a, 0, (wsa, wra, ws2a, wr2a, wg3a, wg4a))
    part_b = Reduction(order_b, 1, (wsb, wrb, ws2b, wr2b, wg3b, wg4b))
    part_a.begin()

    def send_output(tile, c):
        return remote(ob.at[tile, c], outr.at[2 * (h - 1) + tile], ob_send.at[tile, c], ob_recv.at[2 * (h - 1) + tile], pos, c)

    def project():
        for tile in range(2):
            for s in range(4):
                @pl.when(h != s)
                def _():
                    remote(ma.at[tile, s], ma.at[tile, s], ma_send.at[0], ma_recv.at[tile, s], pos, h).wait_recv()
            for c in range(4):
                block = mm(ma[tile, 0], w_v[0:W, c * W:(c + 1) * W])
                for s in range(1, 4):
                    block = block + mm(ma[tile, s], w_v[s * W:(s + 1) * W, c * W:(c + 1) * W])
                ob[tile, c] = block.astype(BF)

                @pl.when(h != c)
                def _():
                    send_output(tile, c).start()

                @pl.when(h == c)
                def _():
                    outr[2 * (h - 1) + tile] = ob[tile, c]

    own_rows = pl.ds(pl.multiple_of(h * W, W), W)
    fg[...] = jnp.zeros_like(fg)

    def backward(t, carry):
        @pl.when(h == 3)
        def _():
            ag_wait_right(3, t)

        @pl.when(h == 0)
        def _():
            ag_wait_left(3, t)

        gmt = mm_nt(w_v[own_rows, 0:W], cot[0, t])
        for s in range(1, 4):
            gmt = gmt + mm_nt(w_v[own_rows, s * W:(s + 1) * W], cot[s, t])
        @pl.when(t == 2)
        def _():
            part_a.to_high()

        @pl.when(t == 3)
        def _():
            part_b.begin()

        gm = gmt.T.astype(BF)
        gmt = gmt.astype(BF).astype(F32)
        q_tile = q_v[t] * jnp.asarray(0.125, BF)
        dqt = []
        for hd in range(4):
            at = slice(hd * 64, (hd + 1) * 64)
            block = slice(hd * 256, (hd + 1) * 256)
            gm_head = gm * head_masks[hd]
            gbd[block, :] = gm_head
            qbd[block, :] = q_tile * head_masks[hd]
            centre = jnp.sum(gmt[at] * mixf[t, at, :], axis=0, keepdims=True)
            grad_probs = mm_nt(vs[t], gm_head)
            dscore = (pt_v[t, :, block].astype(F32) * (grad_probs - centre)).astype(BF)
            dst_v[:, block] = dscore
            dqt.append(mm(kst[t, at, :], dscore))
        gq_v[t] = (jnp.concatenate(dqt, axis=0) * 0.125).T.astype(BF)
        dk = mm(dst_v[...], qbd[...])
        dv = mm(pt_v[t], gbd[...])
        dko[t] = dk[0:256]
        dvo[t] = dv[0:256]
        p0[t] = lanes(dk[256:320], dv[256:320])
        p1[t] = lanes(dk[320:384], dv[320:384])
        fg[...] += lanes(dk[384:768], dv[384:768])
        return carry

    lax.fori_loop(0, 4, backward, 0)

    def level(b):
        return fg[b * 64:(b + 1) * 64, :]

    def cut(buffer, b, parts):
        rows = 64 // parts
        whole = level(b)
        for part in range(parts):
            buffer[part] = stack_kv(whole[part * rows:(part + 1) * rows]).astype(BF)

    e3[...] = stack_kv(level(3)).astype(BF)
    cut(e4, 4, 2)
    cut(e5, 5, 4)

    def down_pair(m, index, s0, r0, s1, r1, s2, r2):
        if m == 1:
            return s0, r0
        if m < 4:
            return s1.at[(index ^ m) & 1], r1.at[m - 2]
        return s2.at[(index ^ m) & 3], r2.at[m - 4]

    dh = []
    for m in range(1, 8):
        src, dst = down_pair(m, g, e3, re3, e4, re4, e5, re5)
        dh.append(remote(src, dst, dh_send.at[m - 1], dh_recv.at[m - 1], pos ^ (8 * m), h))
        dh[-1].start()
    e0[...] = stack_kv(level(0)).astype(BF)
    cut(e1, 1, 2)
    cut(e2, 2, 4)
    dl = []
    for m in range(1, 8):
        src, dst = down_pair(m, i, e0, re0, e1, re1, e2, re2)
        dl.append(remote(src, dst, dl_send.at[m - 1], dl_recv.at[m - 1], pos ^ m, h))
        dl[-1].start()

    part_a.to_back_x()

    @pl.when(middle)
    def _():
        project()

    part_b.to_high()
    part_a.to_back_low()

    for copy in dh:
        copy.wait_recv()

    def f32_kv(x):
        return unstack_kv(x.astype(F32))

    quarter = f32_kv(re5[0]) + f32_kv(re5[1]) + f32_kv(re5[2]) + f32_kv(re5[3])
    half = f32_kv(re4[0]) + f32_kv(re4[1]) + spread2(quarter)
    group_grad = f32_kv(re3[...]) + spread2(half)
    for r in range(8):
        d3s[r] = stack_kv(group_grad[r * 8:(r + 1) * 8]).astype(BF)
    d3 = []
    for m in range(1, 8):
        d3.append(remote(d3s.at[i ^ m], rd3.at[m], d3_send.at[m - 1], d3_recv.at[m - 1], pos ^ m, h))
        d3[-1].start()

    part_b.to_back_x()

    for copy in dl:
        copy.wait_recv()
    for copy in d3:
        copy.wait_recv()
    eighth = f32_kv(d3s[i])
    for m in range(1, 8):
        eighth = eighth + f32_kv(rd3[m])
    quarter = f32_kv(re2[0]) + f32_kv(re2[1]) + f32_kv(re2[2]) + f32_kv(re2[3]) + spread2(eighth)
    half = f32_kv(re1[0]) + f32_kv(re1[1]) + spread2(quarter)
    top_grad = f32_kv(re0[...]) + spread2(half)
    spread_top = spread2(top_grad)
    for n in range(2):
        first = 2 * (1 - n)
        down_1 = p1[first] + p1[first + 1] + spread_top[n * 64:(n + 1) * 64]
        spread_1 = spread2(down_1)
        for r in range(2):
            t = 2 * n + r
            down_0 = p0[t ^ 1] + spread_1[r * 64:(r + 1) * 64]
            back = repeat_rows(down_0, 2) * 0.5
            gk_v[t] = (dko[t] + back[:, :W]).astype(BF)
            gv_v[t] = (dvo[t] + back[:, W:]).astype(BF)
    part_b.to_back_low()
    part_a.finish()
    for t in range(4):
        @pl.when(h != 1 + (t >> 1))
        def _():
            remote(outr.at[t], outr.at[t], ob_send.at[0, 0], ob_recv.at[t], pos, h).wait_recv()
    part_b.finish()

    for copy in up + uh + dl + dh + d3:
        copy.wait_send()
    part_a.wait_sends()
    part_b.wait_sends()
    for t in range(4):
        @pl.when(h != 1 + (t >> 1))
        def _():
            send_mixed(t).wait_send()
    for tile in range(2):
        for c in range(4):
            @pl.when(jnp.logical_and(middle, h != c))
            def _():
                send_output(tile, c).wait_send()
    for k in range(3):
        for c in range(4):
            @pl.when(jnp.logical_and(h - k >= 0, h < 3))
            def _():
                ag_right(k, c).wait_send()

            @pl.when(jnp.logical_and(h + k <= 3, h > 0))
            def _():
                ag_left(k, c).wait_send()


def hand_over(*arrays):
    n = len(arrays)

    def copy_kernel(*refs):
        sems = refs[2 * n]
        copies = [pltpu.make_async_copy(refs[k], refs[n + k], sems.at[k]) for k in range(n)]
        for copy in copies:
            copy.start()
        for copy in copies:
            copy.wait()

    return pl.pallas_call(
        copy_kernel,
        out_shape=[jax.ShapeDtypeStruct(a.shape, a.dtype) for a in arrays],
        in_specs=[pl.BlockSpec(memory_space=pltpu.VMEM)] * n,
        out_specs=[pl.BlockSpec(memory_space=pltpu.HBM)] * n,
        scratch_shapes=[pltpu.SemaphoreType.DMA((n,))],
    )(*[pltpu.with_memory_space_constraint(a, pltpu.VMEM) for a in arrays])


def local(queries, keys, values, out_weight, cotangent):
    tiles = (4, TILE, W)

    def v(*shape, dtype=BF):
        return pltpu.VMEM(shape, dtype)

    def f(*shape):
        return pltpu.VMEM(shape, F32)

    dma = pltpu.SemaphoreType.DMA
    scratch = [
        v(4, 256, 256), v(4, 768, 256), v(4, 768, 256), v(4, 256, 768), v(4, 256, 768),
        v(1024, 1024), v(4, 4, 256, 256), v(4, 768, 1024), v(768, 1024),
        v(4, 256, 256), f(4, 256, 256), v(4, 256, 256), v(2, 4, 256, 256),
        v(2, 4, 256, 256),
        v(1024, 256), v(1024, 256), f(4, 256, 256), f(4, 256, 256),
        f(4, 64, 512), f(4, 64, 512), f(384, 512), f(4, 256, 256),
        v(8, 32, 768), v(8, 32, 768), v(4, 16, 384), v(8, 16, 384), v(4, 16, 384), v(8, 4, 16, 384),
        v(8, 32, 256), v(8, 32, 256), v(4, 16, 128), v(8, 16, 128), v(4, 16, 128), v(8, 4, 16, 128),
        v(144, 256), v(80, 256), v(48, 256), v(144, 256), v(2, 80, 256), v(4, 48, 256),
        f(64, 512), v(128, 256), v(64, 256), v(32, 256),
        v(128, 256), v(2, 64, 256), v(4, 32, 256), v(384, 256), v(384, 256),
        v(128, 256), v(2, 64, 256), v(4, 32, 256), v(128, 256), v(2, 64, 256), v(4, 32, 256),
        v(128, 256), v(2, 64, 256), v(4, 32, 256), v(128, 256), v(2, 64, 256), v(4, 32, 256),
        v(8, 16, 256), v(8, 16, 256),
        dma((14,)), dma((2, 3, 4)), dma((2, 3, 4)),
        dma((7,)), dma((7,)), dma((7,)), dma((7,)),
        dma((4,)), dma((2, 4)), dma((2, 4)), dma((4,)),
    ] + [dma((2, 7))] * 8 + [dma((7,))] * 6
    out_shape = [pltpu.VMEM(tiles, BF)] * 4 + [pltpu.VMEM((256, 1024), F32)]
    output, gq, gk, gv, wg = pl.pallas_call(
        kernel,
        out_shape=out_shape,
        in_specs=[pl.BlockSpec(memory_space=pltpu.HBM)] * 5,
        out_specs=[pl.BlockSpec(memory_space=pltpu.VMEM)] * 5,
        scratch_shapes=scratch,
        compiler_params=pltpu.CompilerParams(
            collective_id=0, has_side_effects=True, vmem_limit_bytes=48 * 1024 * 1024
        ),
    )(*[
        pltpu.with_memory_space_constraint(a, pltpu.HBM)
        for a in (
            queries.reshape(tiles), keys.reshape(tiles), values.reshape(tiles), out_weight,
            cotangent.reshape(tiles),
        )
    ])
    output, gq, gk, gv, wg = hand_over(output, gq, gk, gv, wg)
    rows = queries.shape
    return output.reshape(rows), gq.reshape(rows), gk.reshape(rows), gv.reshape(rows), wg


def solution(mesh):
    in_specs = (P("tile", "head"), P("tile", "head"), P("tile", "head"), P(), P("tile", "head"))
    out_specs = (
        P("tile", "head"),
        P("tile", "head"),
        P("tile", "head"),
        P("tile", "head"),
        P("head", None),
    )
    return jax.shard_map(local, mesh=mesh, in_specs=in_specs, out_specs=out_specs, check_vma=False)
```

```python
import math

import jax
import jax.numpy as jnp
from jax import lax
from jax.experimental import pallas as pl
from jax.experimental.pallas import tpu as pltpu
from jax.sharding import PartitionSpec as P

BF = jnp.bfloat16
F32 = jnp.float32
MESH = pl.DeviceIdType.MESH
ROOT_HALF = 1.0 / math.sqrt(2.0)
NT = (((1,), (1,)), ((), ()))
TILE = 256
W = 256


def mm(a, b):
    return jnp.dot(a, b, preferred_element_type=F32)


def mm_nt(a, b):
    return lax.dot_general(a, b, NT, preferred_element_type=F32)


def iota(shape, axis):
    return lax.broadcasted_iota(jnp.int32, shape, axis)


def ones_where(mask):
    return jnp.where(mask, 1.0, 0.0).astype(BF)


def pool2(x):
    n = x.shape[0]
    pairs = ones_where((iota((n // 2, n), 1) >> 1) == iota((n // 2, n), 0))
    return (mm(pairs, x) * ROOT_HALF).astype(BF)


def repeat_rows(x, times_log2):
    n = x.shape[0]
    big = n << times_log2
    spread = ones_where((iota((big, n), 0) >> times_log2) == iota((big, n), 1))
    high = x.astype(BF)
    low = (x - high.astype(F32)).astype(BF)
    return mm(spread, high) + mm(spread, low)


def spread(x, levels):
    return repeat_rows(x, levels) * ROOT_HALF ** levels


def block(k):
    return pl.ds(pl.multiple_of(k * W, W), W)


def lanes(a, b):
    return jnp.concatenate([a, b], axis=1)


def stack_kv(x):
    return jnp.concatenate([x[:, :W], x[:, W:]], axis=0)


def unstack_kv(x):
    n = x.shape[0] // 2
    return jnp.concatenate([x[:n], x[n:]], axis=1)


def kernel(
    q_hbm, k_hbm, v_hbm, w_hbm, c_hbm,
    outr, gq_v, gk_v, gv_v, wgo,
    q_v, ks, vs, kst, vst, w_v, cot, scores, pt_v, dst_v, mixt, mixf, mixed, ma, ob,
    qbd, gbd, inv, base, p0, p1, fg, wpart, wsa, wra, ws2a, wr2a, wg3a, wg4a,
    wsb, wrb, ws2b, wr2b, wg3b, wg4b,
    u0, u1, u2, ru0, ru1, ru2, n3f, h0, h1, h2, rh0, rh1, rh2, fk, fv,
    e0, e1, e2, e3, e4, e5, re0, re1, re2, re3, re4, re5, d3s, rd3,
    in_sem, ag_send, ag_recv, up_send, up_recv, uh_send, uh_recv,
    ma_send, ma_recv, ob_send, ob_recv,
    w1_send, w1_recv, w2_send, w2_recv, w3_send, w3_recv, w4_send, w4_recv,
    dl_send, dl_recv, dh_send, dh_recv, d3_send, d3_recv,
):
    pos = lax.axis_index("tile")
    h = lax.axis_index("head")
    i = pos & 7
    g = pos >> 3

    in_cot = [pltpu.make_async_copy(c_hbm.at[c], cot.at[block(c), block(h)], in_sem.at[c]) for c in range(4)]
    in_k = [pltpu.make_async_copy(k_hbm.at[t], ks.at[t, pl.ds(0, TILE)], in_sem.at[4 + t]) for t in range(4)]
    in_v = [pltpu.make_async_copy(v_hbm.at[t], vs.at[t, pl.ds(0, TILE)], in_sem.at[8 + t]) for t in range(4)]
    in_q = pltpu.make_async_copy(q_hbm, q_v, in_sem.at[12])
    in_w = pltpu.make_async_copy(w_hbm, w_v, in_sem.at[13])
    for copy in in_k + in_v + in_cot + [in_q, in_w]:
        copy.start()

    barrier = pltpu.get_barrier_semaphore()
    for m in (4, 5, 6, 7, 2, 3, 1):
        pl.semaphore_signal(barrier, inc=1, device_id=(pos ^ (8 * m), h), device_id_type=MESH)
    for m in range(1, 4):
        pl.semaphore_signal(barrier, inc=1, device_id=(pos, h ^ m), device_id_type=MESH)
    for m in range(1, 8):
        pl.semaphore_signal(barrier, inc=1, device_id=(pos ^ m, h), device_id_type=MESH)

    def remote(src, dst, send_sem, recv_sem, to_pos, to_head):
        return pltpu.make_async_remote_copy(
            src_ref=src, dst_ref=dst, send_sem=send_sem, recv_sem=recv_sem,
            device_id=(to_pos, to_head), device_id_type=MESH,
        )

    def ag_copy(way, shard, k, c, to_head):
        part = cot.at[block(c), block(shard)]
        return remote(part, part, ag_send.at[way, k, c], ag_recv.at[way, k, c], pos, to_head)

    def ag_right(k, c):
        return ag_copy(0, h - k, k, c, h + 1)

    def ag_left(k, c):
        return ag_copy(1, h + k, k, c, h - 1)

    def ag_wait_right(k, c):
        ag_copy(0, h - k, k - 1, c, h).wait_recv()

    def ag_wait_left(k, c):
        ag_copy(1, h + k, k - 1, c, h).wait_recv()

    def ag_forward(k, c):
        @pl.when(h - k >= 0)
        def _():
            ag_wait_right(k, c)

            @pl.when(h < 3)
            def _():
                ag_right(k, c).start()

        @pl.when(h + k <= 3)
        def _():
            ag_wait_left(k, c)

            @pl.when(h > 0)
            def _():
                ag_left(k, c).start()

    for copy in in_k + in_v:
        copy.wait()
    quads = ones_where((iota((64, TILE), 1) >> 2) == iota((64, TILE), 0))
    leaf = [
        (mm(quads, lanes(ks[t, 0:TILE, :], vs[t, 0:TILE, :])) * 0.5).astype(BF) for t in range(4)
    ]
    node1 = [pool2(jnp.concatenate([leaf[2 * n], leaf[2 * n + 1]], axis=0)) for n in range(2)]
    top = pool2(jnp.concatenate(node1, axis=0))
    pool_1 = pool2(top)
    pool_2 = pool2(pool_1)
    n = 16
    pairs = ones_where((iota((n // 2, n), 1) >> 1) == iota((n // 2, n), 0))
    pool_3f = (mm(pairs, pool_2) * ROOT_HALF).astype(BF).astype(F32)
    pool_3 = jnp.concatenate([pool_3f[:, :W], pool_3f[:, W:]], axis=0).astype(BF)
    u0[0:128, :] = stack_kv(top)
    u0[128:144, :] = pool_3
    u1[0:64, :] = stack_kv(pool_1)
    u1[64:80, :] = pool_3
    u2[0:32, :] = stack_kv(pool_2)
    u2[32:48, :] = pool_3

    for copy in in_cot:
        copy.wait()
    pl.semaphore_wait(barrier, 17)

    def low_pair(m, s0, r0, s1, r1, s2, r2):
        if m == 1:
            return s0, r0
        if m < 4:
            return s1, r1.at[m - 2]
        return s2, r2.at[m - 4]

    up = []
    for m in range(1, 8):
        src, dst = low_pair(m, u0, ru0, u1, ru1, u2, ru2)
        up.append(remote(src, dst, up_send.at[m - 1], up_recv.at[m - 1], pos ^ m, h))
        up[-1].start()

    for c in range(4):
        @pl.when(h < 3)
        def _():
            ag_right(0, c).start()

        @pl.when(h > 0)
        def _():
            ag_left(0, c).start()

    for t in range(4):
        other = leaf[t ^ 1]
        ks[t, 256:320, :] = other[:, :W]
        vs[t, 256:320, :] = other[:, W:]
        other = node1[(t >> 1) ^ 1]
        ks[t, 320:384, :] = other[:, :W]
        vs[t, 320:384, :] = other[:, W:]
        kst[t, :, 0:384] = ks[t, 0:384, :].T
        vst[t, :, 0:384] = vs[t, 0:384, :].T

    in_q.wait()
    in_w.wait()

    n3f[pl.ds(pl.multiple_of(i * 8, 8), 8), :] = jnp.concatenate([pool_3f[:, :W], pool_3f[:, W:]], axis=1)

    def put_group_part(part, sender):
        part = part.astype(F32)
        n3f[pl.ds(pl.multiple_of(sender * 8, 8), 8), :] = jnp.concatenate([part[0:8], part[8:16]], axis=1)

    for m in range(1, 8):
        up[m - 1].wait_recv()
        sender = i ^ m
        if m == 1:
            fk[0:64, :] = ru0[0:64, :]
            fv[0:64, :] = ru0[64:128, :]
            put_group_part(ru0[128:144, :], sender)
        elif m < 4:
            at = pl.multiple_of(64 + (sender & 1) * 32, 32)
            fk[pl.ds(at, 32), :] = ru1[m - 2, 0:32, :]
            fv[pl.ds(at, 32), :] = ru1[m - 2, 32:64, :]
            put_group_part(ru1[m - 2, 64:80, :], sender)
        else:
            at = pl.multiple_of(128 + (sender & 3) * 16, 16)
            fk[pl.ds(at, 16), :] = ru2[m - 4, 0:16, :]
            fv[pl.ds(at, 16), :] = ru2[m - 4, 16:32, :]
            put_group_part(ru2[m - 4, 32:48, :], sender)
    group_node = n3f[...].astype(BF)
    group_1 = pool2(group_node)
    group_2 = pool2(group_1)
    h0[...] = stack_kv(group_node)
    h1[...] = stack_kv(group_1)
    h2[...] = stack_kv(group_2)
    uh = []
    for m in range(1, 8):
        src, dst = low_pair(m, h0, rh0, h1, rh1, h2, rh2)
        uh.append(remote(src, dst, uh_send.at[m - 1], uh_recv.at[m - 1], pos ^ (8 * m), h))
        uh[-1].start()

    for c in range(4):
        ag_forward(1, c)

    for m in range(1, 8):
        uh[m - 1].wait_recv()
        sender = g ^ m
        if m == 1:
            fk[192:256, :] = rh0[0:64, :]
            fv[192:256, :] = rh0[64:128, :]
        elif m < 4:
            at = pl.multiple_of(256 + (sender & 1) * 32, 32)
            fk[pl.ds(at, 32), :] = rh1[m - 2, 0:32, :]
            fv[pl.ds(at, 32), :] = rh1[m - 2, 32:64, :]
        else:
            at = pl.multiple_of(320 + (sender & 3) * 16, 16)
            fk[pl.ds(at, 16), :] = rh2[m - 4, 0:16, :]
            fv[pl.ds(at, 16), :] = rh2[m - 4, 16:32, :]
    far_kt = fk[...].T
    far_vt = fv[...].T
    for t in range(4):
        ks[t, 384:768, :] = fk[...]
        vs[t, 384:768, :] = fv[...]
        kst[t, :, 384:768] = far_kt
        vst[t, :, 384:768] = far_vt

    head_masks = [ones_where((iota((TILE, W), 1) >> 6) == hd) for hd in range(4)]

    def send_mixed(t):
        return remote(
            mixed.at[t], ma.at[t & 1, :, block(h)], ma_send.at[t], ma_recv.at[t & 1, h], pos, 1 + (t >> 1)
        )

    middle = jnp.logical_and(h > 0, h < 3)

    def forward(step, carry):
        t = (step + 2 * (1 - (h >> 1))) & 3
        q_tile = q_v[t] * jnp.asarray(0.125, BF)

        def scores_of(hd):
            q_head = q_tile * head_masks[hd]
            peak = None
            for lo in (0, 384):
                part = mm_nt(ks[t, lo:lo + 384, :], q_head)
                scores[hd % 2, lo:lo + 384, :] = part
                part = jnp.max(part.reshape(48, 8, 256), axis=0)
                peak = part if peak is None else jnp.maximum(peak, part)
            return jnp.max(peak, axis=0, keepdims=True)

        def weights_of(hd, peak):
            total = None
            for lo in range(0, 768, 128):
                part = jnp.exp(scores[hd % 2, lo:lo + 128, :] - peak)
                pt_v[t, lo:lo + 128, hd * 256:(hd + 1) * 256] = part.astype(BF)
                part = jnp.sum(part.reshape(16, 8, 256), axis=0)
                total = part if total is None else total + part
            inv[t, hd:hd + 1, :] = 1.0 / jnp.sum(total, axis=0, keepdims=True)

        def mix_of(hd):
            at = slice(hd * 64, (hd + 1) * 64)
            mixf[t, at, :] = mm(vst[t, at, :], pt_v[t, :, hd * 256:(hd + 1) * 256]) * inv[t, hd:hd + 1, :]

        peak = scores_of(0)
        for hd in range(4):
            following = scores_of(hd + 1) if hd < 3 else None
            weights_of(hd, peak)
            peak = following
            if hd > 0:
                mix_of(hd - 1)
        mix_of(3)
        whole = mixf[t]
        mixt[:, block(t)] = whole.astype(BF)
        mixed[t] = whole.T.astype(BF)

        owner = 1 + (t >> 1)

        @pl.when(h != owner)
        def _():
            send_mixed(t).start()

        @pl.when(h == owner)
        def _():
            ma[t & 1, :, block(h)] = mixed[t]

        ag_forward(2, step)
        return carry

    lax.fori_loop(0, 4, forward, 0)

    upper = h >> 1
    order_a = (h, h ^ 1, 2 - upper)
    order_b = (3 * (1 - upper),)

    class Reduction:
        def __init__(self, order, part, bufs):
            self.order, self.part, self.nb = order, part, len(order)
            self.ws, self.wr, self.ws2, self.wr2, self.wg3, self.wg4 = bufs
            self.first = 0 if part == 0 else 3

        def begin(self):
            for j, s in enumerate(self.order):
                part = mm(mixt[...], cot[:, block(s)])
                wpart[self.first + j] = part
                for r in range(8):
                    self.ws[r, :, j * W:(j + 1) * W] = part[r * 32:(r + 1) * 32].astype(BF)
            for copy in self.low():
                copy.start()

        def low(self):
            return [
                remote(self.ws.at[i ^ m], self.wr.at[m], w1_send.at[self.part, m - 1], w1_recv.at[self.part, m - 1], pos ^ m, h)
                for m in range(1, 8)
            ]

        def high(self):
            return [
                remote(self.ws2.at[(g ^ m) & 3], self.wr2.at[g], w2_send.at[self.part, m - 1], w2_recv.at[self.part, m - 1],
                       pos ^ (8 * m), h)
                for m in range(1, 8)
            ]

        def back_x(self):
            return [
                remote(self.wg3.at[g & 3], self.wg3.at[g & 3], w3_send.at[self.part, m - 1], w3_recv.at[self.part, m - 1],
                       pos ^ (8 * m), h)
                for m in range(1, 4)
            ]

        def back_low(self):
            return [
                remote(self.wg3, self.wg4.at[m], w4_send.at[self.part, m - 1], w4_recv.at[self.part, m - 1], pos ^ m, h)
                for m in range(1, 8)
            ]

        def to_high(self):
            for copy in self.low():
                copy.wait_recv()
            half = self.nb * 128
            rows = pl.ds(pl.multiple_of(i * 32, 32), 32)
            total = jnp.concatenate([wpart[self.first + j, rows, :] for j in range(self.nb)], axis=1)
            for m in range(1, 8):
                total = total + self.wr[m].astype(F32)
            for r in range(4):
                piece = total[r * 8:(r + 1) * 8]
                self.ws2[r] = jnp.concatenate([piece[:, :half], piece[:, half:]], axis=0).astype(BF)
            for copy in self.high():
                copy.start()
            self.wr2[g] = self.ws2[g & 3]

        def to_back_x(self):
            for m in range(1, 8):
                remote(self.ws2.at[0], self.wr2.at[g ^ m], w2_send.at[self.part, m - 1], w2_recv.at[self.part, m - 1], pos, h).wait_recv()
            total = self.wr2[0].astype(F32)
            for r in range(1, 8):
                total = total + self.wr2[r].astype(F32)
            self.wg3[g & 3] = total.astype(BF)
            for copy in self.back_x():
                copy.start()

        def to_back_low(self):
            for m in range(1, 4):
                slot = self.wg3.at[(g ^ m) & 3]
                remote(slot, slot, w3_send.at[self.part, m - 1], w3_recv.at[self.part, m - 1], pos, h).wait_recv()
            for copy in self.back_low():
                copy.start()
            self.wg4[0] = self.wg3[...]

        def finish(self):
            for copy in self.back_low():
                copy.wait_recv()
            half = self.nb * 128

            def put(m, carry):
                for r in range(4):
                    rows = pl.ds(pl.multiple_of((i ^ m) * 32 + r * 8, 8), 8)
                    piece = self.wg4[m, r].astype(F32)
                    for c in range(2 * self.nb):
                        top, lane = (c * 128) // half, (c * 128) % half
                        columns = pl.ds(pl.multiple_of(self.order[c // 2] * W + (c % 2) * 128, 128), 128)
                        wgo[rows, columns] = piece[top * 8:(top + 1) * 8, lane:lane + 128]
                return carry

            lax.fori_loop(0, 8, put, 0)

        def wait_sends(self):
            for copy in self.low() + self.high() + self.back_x() + self.back_low():
                copy.wait_send()

    part_a = Reduction(order_a, 0, (wsa, wra, ws2a, wr2a, wg3a, wg4a))
    part_b = Reduction(order_b, 1, (wsb, wrb, ws2b, wr2b, wg3b, wg4b))
    part_a.begin()

    def send_output(tile, c):
        return remote(ob.at[tile, c], outr.at[2 * (h - 1) + tile], ob_send.at[tile, c], ob_recv.at[2 * (h - 1) + tile], pos, c)

    def project():
        for tile in range(2):
            for s in range(4):
                @pl.when(h != s)
                def _():
                    part = ma.at[tile, :, block(s)]
                    remote(part, part, ma_send.at[0], ma_recv.at[tile, s], pos, h).wait_recv()
            for c in range(4):
                ob[tile, c] = mm(ma[tile], w_v[:, c * W:(c + 1) * W]).astype(BF)

                @pl.when(h != c)
                def _():
                    send_output(tile, c).start()

                @pl.when(h == c)
                def _():
                    outr[2 * (h - 1) + tile] = ob[tile, c]

    fg[...] = jnp.zeros_like(fg)

    def backward(t, carry):
        @pl.when(h == 3)
        def _():
            ag_wait_right(3, t)

        @pl.when(h == 0)
        def _():
            ag_wait_left(3, t)

        gmt = mm_nt(w_v[block(h), :], cot[block(t), :])
        gmt = jnp.concatenate(
            [gmt[hd * 64:(hd + 1) * 64] * inv[t, hd:hd + 1, :] for hd in range(4)], axis=0
        )
        @pl.when(t == 2)
        def _():
            part_a.to_high()

        @pl.when(t == 3)
        def _():
            part_b.begin()

        gm = gmt.T.astype(BF)
        gmt = gmt.astype(BF).astype(F32)
        q_tile = q_v[t] * jnp.asarray(0.125, BF)
        for hd in range(4):
            part = slice(hd * 256, (hd + 1) * 256)
            gbd[part, :] = gm * head_masks[hd]
            qbd[part, :] = q_tile * head_masks[hd]
        for hd in range(4):
            at = slice(hd * 64, (hd + 1) * 64)
            part = slice(hd * 256, (hd + 1) * 256)
            centre = jnp.sum(gmt[at] * mixf[t, at, :], axis=0, keepdims=True)
            for lo in range(0, 768, 256):
                rows = slice(lo, lo + 256)
                grad_probs = mm_nt(vs[t, rows, :], gbd[part, :])
                dst_v[rows, part] = (pt_v[t, rows, part].astype(F32) * (grad_probs - centre)).astype(BF)
        dqt = []
        for hd in range(4):
            at = slice(hd * 64, (hd + 1) * 64)
            dqt.append(mm(kst[t, at, :], dst_v[:, hd * 256:(hd + 1) * 256]))
        gq_v[t] = (jnp.concatenate(dqt, axis=0) * 0.125).T.astype(BF)
        dk = mm(dst_v[0:384, :], qbd[...])
        dv = mm(pt_v[t, 0:384, :], gbd[...])
        base[t] = lanes(dk[0:256], dv[0:256])
        p0[t] = lanes(dk[256:320], dv[256:320])
        p1[t] = lanes(dk[320:384], dv[320:384])
        fg[:, :W] += mm(dst_v[384:768, :], qbd[...])
        fg[:, W:] += mm(pt_v[t, 384:768, :], gbd[...])
        return carry

    lax.fori_loop(0, 4, backward, 0)

    def level(b):
        return fg[b * 64:(b + 1) * 64, :]

    def cut(buffer, b, parts):
        rows = 64 // parts
        whole = level(b)
        for part in range(parts):
            buffer[part] = stack_kv(whole[part * rows:(part + 1) * rows]).astype(BF)

    e3[...] = stack_kv(level(3)).astype(BF)
    cut(e4, 4, 2)
    cut(e5, 5, 4)

    def down_pair(m, index, s0, r0, s1, r1, s2, r2):
        if m == 1:
            return s0, r0
        if m < 4:
            return s1.at[(index ^ m) & 1], r1.at[m - 2]
        return s2.at[(index ^ m) & 3], r2.at[m - 4]

    dh = []
    for m in range(1, 8):
        src, dst = down_pair(m, g, e3, re3, e4, re4, e5, re5)
        dh.append(remote(src, dst, dh_send.at[m - 1], dh_recv.at[m - 1], pos ^ (8 * m), h))
        dh[-1].start()
    e0[...] = stack_kv(level(0)).astype(BF)
    cut(e1, 1, 2)
    cut(e2, 2, 4)
    dl = []
    for m in range(1, 8):
        src, dst = down_pair(m, i, e0, re0, e1, re1, e2, re2)
        dl.append(remote(src, dst, dl_send.at[m - 1], dl_recv.at[m - 1], pos ^ m, h))
        dl[-1].start()

    part_a.to_back_x()
    part_b.to_high()

    @pl.when(middle)
    def _():
        project()

    def f32_kv(x):
        return unstack_kv(x.astype(F32))

    def total_of(buffer, count):
        total = f32_kv(buffer[0])
        for k in range(1, count):
            total = total + f32_kv(buffer[k])
        return total

    for copy in dl:
        copy.wait_recv()
    top_grad = f32_kv(re0[...]) + spread(total_of(re1, 2), 1) + spread(total_of(re2, 4), 2)
    for n in range(2):
        first = 2 * (1 - n)
        down_1 = p1[first] + p1[first + 1] + spread(top_grad[n * 32:(n + 1) * 32], 1)
        for r in range(2):
            t = 2 * n + r
            down_0 = p0[t ^ 1] + spread(down_1[r * 32:(r + 1) * 32], 1)
            base[t] += repeat_rows(down_0, 2) * 0.5
    part_a.to_back_low()

    for copy in dh:
        copy.wait_recv()

    group_grad = f32_kv(re3[...]) + spread(total_of(re4, 2), 1) + spread(total_of(re5, 4), 2)
    for r in range(8):
        d3s[r] = stack_kv(group_grad[r * 8:(r + 1) * 8]).astype(BF)
    d3 = []
    for m in range(1, 8):
        d3.append(remote(d3s.at[i ^ m], rd3.at[m], d3_send.at[m - 1], d3_recv.at[m - 1], pos ^ m, h))
        d3[-1].start()

    part_b.to_back_x()

    for copy in d3:
        copy.wait_recv()
    eighth = f32_kv(d3s[i])
    for m in range(1, 8):
        eighth = eighth + f32_kv(rd3[m])
    eighth = eighth * (0.25 * ROOT_HALF ** 3)
    for t in range(4):
        for half in range(2):
            rows = slice(half * 128, (half + 1) * 128)
            whole = base[t, rows, :] + eighth[2 * t + half:2 * t + half + 1, :]
            gk_v[t, rows, :] = whole[:, :W].astype(BF)
            gv_v[t, rows, :] = whole[:, W:].astype(BF)
    part_b.to_back_low()
    part_a.finish()
    for t in range(4):
        @pl.when(h != 1 + (t >> 1))
        def _():
            remote(outr.at[t], outr.at[t], ob_send.at[0, 0], ob_recv.at[t], pos, h).wait_recv()
    part_b.finish()

    for copy in up + uh + dl + dh + d3:
        copy.wait_send()
    part_a.wait_sends()
    part_b.wait_sends()
    for t in range(4):
        @pl.when(h != 1 + (t >> 1))
        def _():
            send_mixed(t).wait_send()
    for tile in range(2):
        for c in range(4):
            @pl.when(jnp.logical_and(middle, h != c))
            def _():
                send_output(tile, c).wait_send()
    for k in range(3):
        for c in range(4):
            @pl.when(jnp.logical_and(h - k >= 0, h < 3))
            def _():
                ag_right(k, c).wait_send()

            @pl.when(jnp.logical_and(h + k <= 3, h > 0))
            def _():
                ag_left(k, c).wait_send()


def hand_over(*arrays):
    n = len(arrays)

    def copy_kernel(*refs):
        sems = refs[2 * n]
        copies = [pltpu.make_async_copy(refs[k], refs[n + k], sems.at[k]) for k in range(n)]
        for copy in copies:
            copy.start()
        for copy in copies:
            copy.wait()

    return pl.pallas_call(
        copy_kernel,
        out_shape=[jax.ShapeDtypeStruct(a.shape, a.dtype) for a in arrays],
        in_specs=[pl.BlockSpec(memory_space=pltpu.VMEM)] * n,
        out_specs=[pl.BlockSpec(memory_space=pltpu.HBM)] * n,
        scratch_shapes=[pltpu.SemaphoreType.DMA((n,))],
    )(*[pltpu.with_memory_space_constraint(a, pltpu.VMEM) for a in arrays])


def local(queries, keys, values, out_weight, cotangent):
    tiles = (4, TILE, W)

    def v(*shape, dtype=BF):
        return pltpu.VMEM(shape, dtype)

    def f(*shape):
        return pltpu.VMEM(shape, F32)

    dma = pltpu.SemaphoreType.DMA
    scratch = [
        v(4, 256, 256), v(4, 768, 256), v(4, 768, 256), v(4, 256, 768), v(4, 256, 768),
        v(1024, 1024), v(1024, 1024), f(2, 768, 256), v(4, 768, 1024), v(768, 1024),
        v(256, 1024), f(4, 256, 256), v(4, 256, 256), v(2, 256, 1024),
        v(2, 4, 256, 256),
        v(1024, 256), v(1024, 256), f(4, 8, 256), f(4, 256, 512),
        f(4, 64, 512), f(4, 64, 512), f(384, 512), f(4, 256, 256),
        v(8, 32, 768), v(8, 32, 768), v(4, 16, 384), v(8, 16, 384), v(4, 16, 384), v(8, 4, 16, 384),
        v(8, 32, 256), v(8, 32, 256), v(4, 16, 128), v(8, 16, 128), v(4, 16, 128), v(8, 4, 16, 128),
        v(144, 256), v(80, 256), v(48, 256), v(144, 256), v(2, 80, 256), v(4, 48, 256),
        f(64, 512), v(128, 256), v(64, 256), v(32, 256),
        v(128, 256), v(2, 64, 256), v(4, 32, 256), v(384, 256), v(384, 256),
        v(128, 256), v(2, 64, 256), v(4, 32, 256), v(128, 256), v(2, 64, 256), v(4, 32, 256),
        v(128, 256), v(2, 64, 256), v(4, 32, 256), v(128, 256), v(2, 64, 256), v(4, 32, 256),
        v(8, 16, 256), v(8, 16, 256),
        dma((14,)), dma((2, 3, 4)), dma((2, 3, 4)),
        dma((7,)), dma((7,)), dma((7,)), dma((7,)),
        dma((4,)), dma((2, 4)), dma((2, 4)), dma((4,)),
    ] + [dma((2, 7))] * 8 + [dma((7,))] * 6
    out_shape = [pltpu.VMEM(tiles, BF)] * 4 + [pltpu.VMEM((256, 1024), F32)]
    output, gq, gk, gv, wg = pl.pallas_call(
        kernel,
        out_shape=out_shape,
        in_specs=[pl.BlockSpec(memory_space=pltpu.HBM)] * 5,
        out_specs=[pl.BlockSpec(memory_space=pltpu.VMEM)] * 5,
        scratch_shapes=scratch,
        compiler_params=pltpu.CompilerParams(
            collective_id=0, has_side_effects=True, vmem_limit_bytes=48 * 1024 * 1024
        ),
    )(*[
        pltpu.with_memory_space_constraint(a, pltpu.HBM)
        for a in (
            queries.reshape(tiles), keys.reshape(tiles), values.reshape(tiles), out_weight,
            cotangent.reshape(tiles),
        )
    ])
    output, gq, gk, gv, wg = hand_over(output, gq, gk, gv, wg)
    rows = queries.shape
    return output.reshape(rows), gq.reshape(rows), gk.reshape(rows), gv.reshape(rows), wg


def solution(mesh):
    in_specs = (P("tile", "head"), P("tile", "head"), P("tile", "head"), P(), P("tile", "head"))
    out_specs = (
        P("tile", "head"),
        P("tile", "head"),
        P("tile", "head"),
        P("tile", "head"),
        P("head", None),
    )
    return jax.shard_map(local, mesh=mesh, in_specs=in_specs, out_specs=out_specs, check_vma=False)
```

```python
import math

import jax
import jax.numpy as jnp
from jax import lax
from jax.experimental import pallas as pl
from jax.experimental.pallas import tpu as pltpu
from jax.sharding import PartitionSpec as P

BF = jnp.bfloat16
F32 = jnp.float32
MESH = pl.DeviceIdType.MESH
ROOT_HALF = 1.0 / math.sqrt(2.0)
NT = (((1,), (1,)), ((), ()))
TILE = 256
W = 256


def mm(a, b):
    return jnp.dot(a, b, preferred_element_type=F32)


def mm_nt(a, b):
    return lax.dot_general(a, b, NT, preferred_element_type=F32)


def iota(shape, axis):
    return lax.broadcasted_iota(jnp.int32, shape, axis)


def ones_where(mask):
    return jnp.where(mask, 1.0, 0.0).astype(BF)


def pool2(x):
    n = x.shape[0]
    pairs = ones_where((iota((n // 2, n), 1) >> 1) == iota((n // 2, n), 0))
    return (mm(pairs, x) * ROOT_HALF).astype(BF)


def repeat_rows(x, times_log2):
    n = x.shape[0]
    big = n << times_log2
    spread = ones_where((iota((big, n), 0) >> times_log2) == iota((big, n), 1))
    high = x.astype(BF)
    low = (x - high.astype(F32)).astype(BF)
    return mm(spread, high) + mm(spread, low)


def spread(x, levels):
    return repeat_rows(x, levels) * ROOT_HALF ** levels


def block(k):
    return pl.ds(pl.multiple_of(k * W, W), W)


def lanes(a, b):
    return jnp.concatenate([a, b], axis=1)


def stack_kv(x):
    return jnp.concatenate([x[:, :W], x[:, W:]], axis=0)


def unstack_kv(x):
    n = x.shape[0] // 2
    return jnp.concatenate([x[:n], x[n:]], axis=1)


def kernel(
    q_hbm, k_hbm, v_hbm, w_hbm, c_hbm,
    outr, gq_v, gk_v, gv_v, wgo,
    q_v, ks, vs, kst, vst, w_v, cot, scores, pt_v, dst_v, mixt, mixf, mixed, ma, ob,
    qbd, gbd, inv, base, p0, p1, fg, wpart, wsa, wra, ws2a, wr2a, wg3a, wg4a,
    wsb, wrb, ws2b, wr2b, wg3b, wg4b,
    u0, u1, u2, ru0, ru1, ru2, n3f, h0, h1, h2, rh0, rh1, rh2, fk, fv,
    e0, e1, e2, e3, e4, e5, re0, re1, re2, re3, re4, re5, d3s, rd3,
    in_sem, ag_send, ag_recv, up_send, up_recv, uh_send, uh_recv,
    ma_send, ma_recv, ob_send, ob_recv,
    w1_send, w1_recv, w2_send, w2_recv, w3_send, w3_recv, w4_send, w4_recv,
    dl_send, dl_recv, dh_send, dh_recv, d3_send, d3_recv,
):
    pos = lax.axis_index("tile")
    h = lax.axis_index("head")
    i = pos & 7
    g = pos >> 3

    in_cot = [pltpu.make_async_copy(c_hbm.at[c], cot.at[block(c), block(h)], in_sem.at[c]) for c in range(4)]
    in_k = [pltpu.make_async_copy(k_hbm.at[t], ks.at[t, pl.ds(0, TILE)], in_sem.at[4 + t]) for t in range(4)]
    in_v = [pltpu.make_async_copy(v_hbm.at[t], vs.at[t, pl.ds(0, TILE)], in_sem.at[8 + t]) for t in range(4)]
    in_q = pltpu.make_async_copy(q_hbm, q_v, in_sem.at[12])
    in_w = pltpu.make_async_copy(w_hbm, w_v, in_sem.at[13])
    for copy in in_k + in_v + in_cot + [in_q, in_w]:
        copy.start()

    barrier = pltpu.get_barrier_semaphore()
    for m in (4, 5, 6, 7, 2, 3, 1):
        pl.semaphore_signal(barrier, inc=1, device_id=(pos ^ (8 * m), h), device_id_type=MESH)
    for m in range(1, 4):
        pl.semaphore_signal(barrier, inc=1, device_id=(pos, h ^ m), device_id_type=MESH)
    for m in range(1, 8):
        pl.semaphore_signal(barrier, inc=1, device_id=(pos ^ m, h), device_id_type=MESH)

    def remote(src, dst, send_sem, recv_sem, to_pos, to_head):
        return pltpu.make_async_remote_copy(
            src_ref=src, dst_ref=dst, send_sem=send_sem, recv_sem=recv_sem,
            device_id=(to_pos, to_head), device_id_type=MESH,
        )

    def ag_copy(way, shard, k, c, to_head):
        part = cot.at[block(c), block(shard)]
        return remote(part, part, ag_send.at[way, k, c], ag_recv.at[way, k, c], pos, to_head)

    def ag_right(k, c):
        return ag_copy(0, h - k, k, c, h + 1)

    def ag_left(k, c):
        return ag_copy(1, h + k, k, c, h - 1)

    def ag_wait_right(k, c):
        ag_copy(0, h - k, k - 1, c, h).wait_recv()

    def ag_wait_left(k, c):
        ag_copy(1, h + k, k - 1, c, h).wait_recv()

    def ag_forward(k, c):
        @pl.when(h - k >= 0)
        def _():
            ag_wait_right(k, c)

            @pl.when(h < 3)
            def _():
                ag_right(k, c).start()

        @pl.when(h + k <= 3)
        def _():
            ag_wait_left(k, c)

            @pl.when(h > 0)
            def _():
                ag_left(k, c).start()

    for copy in in_k + in_v:
        copy.wait()
    quads = ones_where((iota((64, TILE), 1) >> 2) == iota((64, TILE), 0))
    leaf = [
        (mm(quads, lanes(ks[t, 0:TILE, :], vs[t, 0:TILE, :])) * 0.5).astype(BF) for t in range(4)
    ]
    node1 = [pool2(jnp.concatenate([leaf[2 * n], leaf[2 * n + 1]], axis=0)) for n in range(2)]
    top = pool2(jnp.concatenate(node1, axis=0))
    pool_1 = pool2(top)
    pool_2 = pool2(pool_1)
    n = 16
    pairs = ones_where((iota((n // 2, n), 1) >> 1) == iota((n // 2, n), 0))
    pool_3f = (mm(pairs, pool_2) * ROOT_HALF).astype(BF).astype(F32)
    pool_3 = jnp.concatenate([pool_3f[:, :W], pool_3f[:, W:]], axis=0).astype(BF)
    u0[0:128, :] = stack_kv(top)
    u0[128:144, :] = pool_3
    u1[0:64, :] = stack_kv(pool_1)
    u1[64:80, :] = pool_3
    u2[0:32, :] = stack_kv(pool_2)
    u2[32:48, :] = pool_3

    for copy in in_cot:
        copy.wait()
    pl.semaphore_wait(barrier, 17)

    for c in range(4):
        @pl.when(h < 3)
        def _():
            ag_right(0, c).start()

        @pl.when(h > 0)
        def _():
            ag_left(0, c).start()

    def low_pair(m, s0, r0, s1, r1, s2, r2):
        if m == 1:
            return s0, r0
        if m < 4:
            return s1, r1.at[m - 2]
        return s2, r2.at[m - 4]

    up = []
    for m in range(1, 8):
        src, dst = low_pair(m, u0, ru0, u1, ru1, u2, ru2)
        up.append(remote(src, dst, up_send.at[m - 1], up_recv.at[m - 1], pos ^ m, h))
        up[-1].start()

    for t in range(4):
        other = leaf[t ^ 1]
        ks[t, 256:320, :] = other[:, :W]
        vs[t, 256:320, :] = other[:, W:]
        other = node1[(t >> 1) ^ 1]
        ks[t, 320:384, :] = other[:, :W]
        vs[t, 320:384, :] = other[:, W:]
        kst[t, :, 0:384] = ks[t, 0:384, :].T
        vst[t, :, 0:384] = vs[t, 0:384, :].T

    in_q.wait()
    in_w.wait()

    n3f[pl.ds(pl.multiple_of(i * 8, 8), 8), :] = jnp.concatenate([pool_3f[:, :W], pool_3f[:, W:]], axis=1)

    def put_group_part(part, sender):
        part = part.astype(F32)
        n3f[pl.ds(pl.multiple_of(sender * 8, 8), 8), :] = jnp.concatenate([part[0:8], part[8:16]], axis=1)

    for m in range(1, 8):
        up[m - 1].wait_recv()
        sender = i ^ m
        if m == 1:
            fk[0:64, :] = ru0[0:64, :]
            fv[0:64, :] = ru0[64:128, :]
            put_group_part(ru0[128:144, :], sender)
        elif m < 4:
            at = pl.multiple_of(64 + (sender & 1) * 32, 32)
            fk[pl.ds(at, 32), :] = ru1[m - 2, 0:32, :]
            fv[pl.ds(at, 32), :] = ru1[m - 2, 32:64, :]
            put_group_part(ru1[m - 2, 64:80, :], sender)
        else:
            at = pl.multiple_of(128 + (sender & 3) * 16, 16)
            fk[pl.ds(at, 16), :] = ru2[m - 4, 0:16, :]
            fv[pl.ds(at, 16), :] = ru2[m - 4, 16:32, :]
            put_group_part(ru2[m - 4, 32:48, :], sender)
    group_node = n3f[...].astype(BF)
    group_1 = pool2(group_node)
    group_2 = pool2(group_1)
    h0[...] = stack_kv(group_node)
    h1[...] = stack_kv(group_1)
    h2[...] = stack_kv(group_2)
    uh = []
    for m in range(1, 8):
        src, dst = low_pair(m, h0, rh0, h1, rh1, h2, rh2)
        uh.append(remote(src, dst, uh_send.at[m - 1], uh_recv.at[m - 1], pos ^ (8 * m), h))
        uh[-1].start()

    for c in range(4):
        ag_forward(1, c)

    for m in range(1, 8):
        uh[m - 1].wait_recv()
        sender = g ^ m
        if m == 1:
            fk[192:256, :] = rh0[0:64, :]
            fv[192:256, :] = rh0[64:128, :]
        elif m < 4:
            at = pl.multiple_of(256 + (sender & 1) * 32, 32)
            fk[pl.ds(at, 32), :] = rh1[m - 2, 0:32, :]
            fv[pl.ds(at, 32), :] = rh1[m - 2, 32:64, :]
        else:
            at = pl.multiple_of(320 + (sender & 3) * 16, 16)
            fk[pl.ds(at, 16), :] = rh2[m - 4, 0:16, :]
            fv[pl.ds(at, 16), :] = rh2[m - 4, 16:32, :]
    far_kt = fk[...].T
    far_vt = fv[...].T
    for t in range(4):
        ks[t, 384:768, :] = fk[...]
        vs[t, 384:768, :] = fv[...]
        kst[t, :, 384:768] = far_kt
        vst[t, :, 384:768] = far_vt

    head_masks = [ones_where((iota((TILE, W), 1) >> 6) == hd) for hd in range(4)]

    def send_mixed(t):
        return remote(
            mixed.at[t], ma.at[t & 1, :, block(h)], ma_send.at[t], ma_recv.at[t & 1, h], pos, 1 + (t >> 1)
        )

    middle = jnp.logical_and(h > 0, h < 3)

    def forward(step, carry):
        t = (step + 2 * (1 - (h >> 1))) & 3
        q_tile = q_v[t] * jnp.asarray(0.125, BF)

        def scores_of(hd):
            q_head = q_tile * head_masks[hd]
            peak = None
            for lo in (0, 384):
                part = mm_nt(ks[t, lo:lo + 384, :], q_head)
                scores[hd % 2, lo:lo + 384, :] = part
                part = jnp.max(part.reshape(48, 8, 256), axis=0)
                peak = part if peak is None else jnp.maximum(peak, part)
            return jnp.max(peak, axis=0, keepdims=True)

        def weights_of(hd, peak):
            total = None
            for lo in range(0, 768, 128):
                part = jnp.exp(scores[hd % 2, lo:lo + 128, :] - peak)
                pt_v[t, lo:lo + 128, hd * 256:(hd + 1) * 256] = part.astype(BF)
                part = jnp.sum(part.reshape(16, 8, 256), axis=0)
                total = part if total is None else total + part
            inv[t, hd:hd + 1, :] = 1.0 / jnp.sum(total, axis=0, keepdims=True)

        def mix_of(hd):
            at = slice(hd * 64, (hd + 1) * 64)
            mixf[t, at, :] = mm(vst[t, at, :], pt_v[t, :, hd * 256:(hd + 1) * 256]) * inv[t, hd:hd + 1, :]

        peak = scores_of(0)
        for hd in range(4):
            following = scores_of(hd + 1) if hd < 3 else None
            weights_of(hd, peak)
            peak = following
            if hd > 0:
                mix_of(hd - 1)
        mix_of(3)
        whole = mixf[t]
        mixt[:, block(t)] = whole.astype(BF)
        mixed[t] = whole.T.astype(BF)

        owner = 1 + (t >> 1)

        @pl.when(h != owner)
        def _():
            send_mixed(t).start()

        @pl.when(h == owner)
        def _():
            ma[t & 1, :, block(h)] = mixed[t]

        @pl.when(jnp.logical_and(middle, step > 0))
        def _():
            ag_forward(2, step - 1)

        return carry

    lax.fori_loop(0, 4, forward, 0)

    upper = h >> 1
    order_a = (h, h ^ 1, 2 - upper)
    order_b = (3 * (1 - upper),)

    class Reduction:
        def __init__(self, order, part, bufs):
            self.order, self.part, self.nb = order, part, len(order)
            self.ws, self.wr, self.ws2, self.wr2, self.wg3, self.wg4 = bufs
            self.first = 0 if part == 0 else 3

        def begin(self):
            for j, s in enumerate(self.order):
                part = mm(mixt[...], cot[:, block(s)])
                wpart[self.first + j] = part
                for r in range(8):
                    self.ws[r, :, j * W:(j + 1) * W] = part[r * 32:(r + 1) * 32].astype(BF)
            for copy in self.low():
                copy.start()

        def low(self):
            return [
                remote(self.ws.at[i ^ m], self.wr.at[m], w1_send.at[self.part, m - 1], w1_recv.at[self.part, m - 1], pos ^ m, h)
                for m in range(1, 8)
            ]

        def high(self):
            return [
                remote(self.ws2.at[(g ^ m) & 3], self.wr2.at[g], w2_send.at[self.part, m - 1], w2_recv.at[self.part, m - 1],
                       pos ^ (8 * m), h)
                for m in range(1, 8)
            ]

        def back_x(self):
            return [
                remote(self.wg3.at[g & 3], self.wg3.at[g & 3], w3_send.at[self.part, m - 1], w3_recv.at[self.part, m - 1],
                       pos ^ (8 * m), h)
                for m in range(1, 4)
            ]

        def back_low(self):
            return [
                remote(self.wg3, self.wg4.at[m], w4_send.at[self.part, m - 1], w4_recv.at[self.part, m - 1], pos ^ m, h)
                for m in range(1, 8)
            ]

        def to_high(self):
            for copy in self.low():
                copy.wait_recv()
            half = self.nb * 128
            rows = pl.ds(pl.multiple_of(i * 32, 32), 32)
            total = jnp.concatenate([wpart[self.first + j, rows, :] for j in range(self.nb)], axis=1)
            for m in range(1, 8):
                total = total + self.wr[m].astype(F32)
            for r in range(4):
                piece = total[r * 8:(r + 1) * 8]
                self.ws2[r] = jnp.concatenate([piece[:, :half], piece[:, half:]], axis=0).astype(BF)
            for copy in self.high():
                copy.start()
            self.wr2[g] = self.ws2[g & 3]

        def to_back_x(self):
            for m in range(1, 8):
                remote(self.ws2.at[0], self.wr2.at[g ^ m], w2_send.at[self.part, m - 1], w2_recv.at[self.part, m - 1], pos, h).wait_recv()
            total = self.wr2[0].astype(F32)
            for r in range(1, 8):
                total = total + self.wr2[r].astype(F32)
            self.wg3[g & 3] = total.astype(BF)
            for copy in self.back_x():
                copy.start()

        def to_back_low(self):
            for m in range(1, 4):
                slot = self.wg3.at[(g ^ m) & 3]
                remote(slot, slot, w3_send.at[self.part, m - 1], w3_recv.at[self.part, m - 1], pos, h).wait_recv()
            for copy in self.back_low():
                copy.start()
            self.wg4[0] = self.wg3[...]

        def finish(self):
            for copy in self.back_low():
                copy.wait_recv()
            half = self.nb * 128

            def put(m, carry):
                for r in range(4):
                    rows = pl.ds(pl.multiple_of((i ^ m) * 32 + r * 8, 8), 8)
                    piece = self.wg4[m, r].astype(F32)
                    for c in range(2 * self.nb):
                        top, lane = (c * 128) // half, (c * 128) % half
                        columns = pl.ds(pl.multiple_of(self.order[c // 2] * W + (c % 2) * 128, 128), 128)
                        wgo[rows, columns] = piece[top * 8:(top + 1) * 8, lane:lane + 128]
                return carry

            lax.fori_loop(0, 8, put, 0)

        def wait_sends(self):
            for copy in self.low() + self.high() + self.back_x():
                copy.wait_send()

        def wait_back(self):
            for copy in self.back_low():
                copy.wait_send()

    class Last(Reduction):
        def high(self):
            return [
                remote(self.ws2, self.wr2.at[g], w2_send.at[self.part, m - 1], w2_recv.at[self.part, m - 1], pos ^ (8 * m), h)
                for m in range(1, 8)
            ]

        def to_high(self):
            for copy in self.low():
                copy.wait_recv()
            total = wpart[self.first, pl.ds(pl.multiple_of(i * 32, 32), 32), :]
            for m in range(1, 8):
                total = total + self.wr[m].astype(F32)
            self.ws2[...] = total.astype(BF)
            for copy in self.high():
                copy.start()
            self.wr2[g] = self.ws2[...]

        def to_back_low(self):
            for m in range(1, 8):
                remote(self.ws2, self.wr2.at[g ^ m], w2_send.at[self.part, m - 1], w2_recv.at[self.part, m - 1], pos, h).wait_recv()
            total = self.wr2[0].astype(F32)
            for r in range(1, 8):
                total = total + self.wr2[r].astype(F32)
            self.wg3[...] = total.astype(BF)
            for copy in self.back_low():
                copy.start()
            self.wg4[0] = self.wg3[...]

        def finish(self):
            for copy in self.back_low():
                copy.wait_recv()
            for m in range(8):
                wgo[pl.ds(pl.multiple_of((i ^ m) * 32, 32), 32), block(self.order[0])] = self.wg4[m].astype(F32)

        def wait_sends(self):
            for copy in self.low() + self.high():
                copy.wait_send()

    part_a = Reduction(order_a, 0, (wsa, wra, ws2a, wr2a, wg3a, wg4a))
    part_b = Last(order_b, 1, (wsb, wrb, ws2b, wr2b, wg3b, wg4b))

    @pl.when(jnp.logical_not(middle))
    def _():
        for c in range(4):
            ag_forward(2, c)

    part_a.begin()

    @pl.when(middle)
    def _():
        ag_forward(2, 3)

    def send_output(tile, c):
        return remote(ob.at[tile, c], outr.at[2 * (h - 1) + tile], ob_send.at[tile, c], ob_recv.at[2 * (h - 1) + tile], pos, c)

    def send_tile(tile):
        for m in (2, 3, 1):
            send_output(tile, h ^ m).start()

    def project():
        for tile in range(2):
            for s in range(4):
                @pl.when(h != s)
                def _():
                    part = ma.at[tile, :, block(s)]
                    remote(part, part, ma_send.at[0], ma_recv.at[tile, s], pos, h).wait_recv()
        for tile in range(2):
            for c in range(4):
                ob[tile, c] = mm(ma[tile], w_v[:, c * W:(c + 1) * W]).astype(BF)
        for tile in range(2):
            outr[2 * (h - 1) + tile] = ob[tile, h]
        send_tile(0)

    fg[...] = jnp.zeros_like(fg)

    def backward(t, carry):
        @pl.when(h == 3)
        def _():
            ag_wait_right(3, t)

        @pl.when(h == 0)
        def _():
            ag_wait_left(3, t)

        gmt = mm_nt(w_v[block(h), :], cot[block(t), :])
        gmt = jnp.concatenate(
            [gmt[hd * 64:(hd + 1) * 64] * inv[t, hd:hd + 1, :] for hd in range(4)], axis=0
        )
        @pl.when(t == 3 * (1 - (((h + 1) >> 1) & 1)))
        def _():
            part_b.begin()

        gm = gmt.T.astype(BF)
        gmt = gmt.astype(BF).astype(F32)
        q_tile = q_v[t] * jnp.asarray(0.125, BF)
        for hd in range(4):
            part = slice(hd * 256, (hd + 1) * 256)
            gbd[part, :] = gm * head_masks[hd]
            qbd[part, :] = q_tile * head_masks[hd]
        for hd in range(4):
            at = slice(hd * 64, (hd + 1) * 64)
            part = slice(hd * 256, (hd + 1) * 256)
            centre = jnp.sum(gmt[at] * mixf[t, at, :], axis=0, keepdims=True)
            for lo in range(0, 768, 256):
                rows = slice(lo, lo + 256)
                grad_probs = mm_nt(vs[t, rows, :], gbd[part, :])
                dst_v[rows, part] = (pt_v[t, rows, part].astype(F32) * (grad_probs - centre)).astype(BF)
        dqt = []
        for hd in range(4):
            at = slice(hd * 64, (hd + 1) * 64)
            dqt.append(mm(kst[t, at, :], dst_v[:, hd * 256:(hd + 1) * 256]))
        gq_v[t] = (jnp.concatenate(dqt, axis=0) * 0.125).T.astype(BF)
        dk = mm(dst_v[0:384, :], qbd[...])
        dv = mm(pt_v[t, 0:384, :], gbd[...])
        base[t] = lanes(dk[0:256], dv[0:256])
        p0[t] = lanes(dk[256:320], dv[256:320])
        p1[t] = lanes(dk[320:384], dv[320:384])
        fg[:, :W] += mm(dst_v[384:768, :], qbd[...])
        fg[:, W:] += mm(pt_v[t, 384:768, :], gbd[...])

        @pl.when(t == 2)
        def _():
            part_a.to_high()

            @pl.when(middle)
            def _():
                part_b.to_high()

        return carry

    lax.fori_loop(0, 4, backward, 0)

    def level(b):
        return fg[b * 64:(b + 1) * 64, :]

    def cut(buffer, b, parts):
        rows = 64 // parts
        whole = level(b)
        for part in range(parts):
            buffer[part] = stack_kv(whole[part * rows:(part + 1) * rows]).astype(BF)

    e3[...] = stack_kv(level(3)).astype(BF)
    cut(e4, 4, 2)
    cut(e5, 5, 4)

    def down_pair(m, index, s0, r0, s1, r1, s2, r2):
        if m == 1:
            return s0, r0
        if m < 4:
            return s1.at[(index ^ m) & 1], r1.at[m - 2]
        return s2.at[(index ^ m) & 3], r2.at[m - 4]

    dh = []
    for m in range(1, 8):
        src, dst = down_pair(m, g, e3, re3, e4, re4, e5, re5)
        dh.append(remote(src, dst, dh_send.at[m - 1], dh_recv.at[m - 1], pos ^ (8 * m), h))
        dh[-1].start()
    @pl.when(middle)
    def _():
        project()

    @pl.when(jnp.logical_not(middle))
    def _():
        part_b.to_high()

    part_a.to_back_x()
    e0[...] = stack_kv(level(0)).astype(BF)
    cut(e1, 1, 2)
    cut(e2, 2, 4)
    dl = []
    for m in range(1, 8):
        src, dst = down_pair(m, i, e0, re0, e1, re1, e2, re2)
        dl.append(remote(src, dst, dl_send.at[m - 1], dl_recv.at[m - 1], pos ^ m, h))
        dl[-1].start()


    part_a.to_back_low()

    def f32_kv(x):
        return unstack_kv(x.astype(F32))

    def total_of(buffer, count):
        total = f32_kv(buffer[0])
        for k in range(1, count):
            total = total + f32_kv(buffer[k])
        return total

    for copy in up + uh:
        copy.wait_send()
    for t in range(4):
        @pl.when(h != 1 + (t >> 1))
        def _():
            send_mixed(t).wait_send()
    for k in range(3):
        for c in range(4):
            @pl.when(jnp.logical_and(h - k >= 0, h < 3))
            def _():
                ag_right(k, c).wait_send()

            @pl.when(jnp.logical_and(h + k <= 3, h > 0))
            def _():
                ag_left(k, c).wait_send()

    for copy in dh:
        copy.wait_recv()

    group_grad = f32_kv(re3[...]) + spread(total_of(re4, 2), 1) + spread(total_of(re5, 4), 2)
    for r in range(8):
        d3s[r] = stack_kv(group_grad[r * 8:(r + 1) * 8]).astype(BF)
    d3 = []
    for m in range(1, 8):
        d3.append(remote(d3s.at[i ^ m], rd3.at[m], d3_send.at[m - 1], d3_recv.at[m - 1], pos ^ m, h))
        d3[-1].start()

    part_b.to_back_low()

    @pl.when(middle)
    def _():
        send_tile(1)

    for copy in dl:
        copy.wait_recv()
    top_grad = f32_kv(re0[...]) + spread(total_of(re1, 2), 1) + spread(total_of(re2, 4), 2)
    for n in range(2):
        first = 2 * (1 - n)
        down_1 = p1[first] + p1[first + 1] + spread(top_grad[n * 32:(n + 1) * 32], 1)
        for r in range(2):
            t = 2 * n + r
            down_0 = p0[t ^ 1] + spread(down_1[r * 32:(r + 1) * 32], 1)
            base[t] += repeat_rows(down_0, 2) * 0.5

    for copy in dl + dh:
        copy.wait_send()
    part_a.wait_sends()
    part_b.wait_sends()
    for copy in d3:
        copy.wait_recv()
    eighth = f32_kv(d3s[i])
    for m in range(1, 8):
        eighth = eighth + f32_kv(rd3[m])
    eighth = eighth * (0.25 * ROOT_HALF ** 3)
    for t in range(4):
        for half in range(2):
            rows = slice(half * 128, (half + 1) * 128)
            whole = base[t, rows, :] + eighth[2 * t + half:2 * t + half + 1, :]
            gk_v[t, rows, :] = whole[:, :W].astype(BF)
            gv_v[t, rows, :] = whole[:, W:].astype(BF)
    part_a.finish()
    for t in range(4):
        @pl.when(h != 1 + (t >> 1))
        def _():
            remote(outr.at[t], outr.at[t], ob_send.at[0, 0], ob_recv.at[t], pos, h).wait_recv()
    part_b.finish()

    for copy in d3:
        copy.wait_send()
    part_a.wait_back()
    part_b.wait_back()
    for tile in range(2):
        for c in range(4):
            @pl.when(jnp.logical_and(middle, h != c))
            def _():
                send_output(tile, c).wait_send()


def hand_over(*arrays):
    n = len(arrays)

    def copy_kernel(*refs):
        sems = refs[2 * n]
        copies = []
        for k in range(n):
            size = arrays[k].shape[0] // 4
            for part in range(4):
                cut = pl.ds(part * size, size)
                copies.append(pltpu.make_async_copy(refs[k].at[cut], refs[n + k].at[cut], sems.at[k, part]))
        for copy in copies:
            copy.start()
        for copy in copies:
            copy.wait()

    return pl.pallas_call(
        copy_kernel,
        out_shape=[jax.ShapeDtypeStruct(a.shape, a.dtype) for a in arrays],
        in_specs=[pl.BlockSpec(memory_space=pltpu.VMEM)] * n,
        out_specs=[pl.BlockSpec(memory_space=pltpu.HBM)] * n,
        scratch_shapes=[pltpu.SemaphoreType.DMA((n, 4))],
    )(*[pltpu.with_memory_space_constraint(a, pltpu.VMEM) for a in arrays])


def local(queries, keys, values, out_weight, cotangent):
    tiles = (4, TILE, W)

    def v(*shape, dtype=BF):
        return pltpu.VMEM(shape, dtype)

    def f(*shape):
        return pltpu.VMEM(shape, F32)

    dma = pltpu.SemaphoreType.DMA
    scratch = [
        v(4, 256, 256), v(4, 768, 256), v(4, 768, 256), v(4, 256, 768), v(4, 256, 768),
        v(1024, 1024), v(1024, 1024), f(2, 768, 256), v(4, 768, 1024), v(768, 1024),
        v(256, 1024), f(4, 256, 256), v(4, 256, 256), v(2, 256, 1024),
        v(2, 4, 256, 256),
        v(1024, 256), v(1024, 256), f(4, 8, 256), f(4, 256, 512),
        f(4, 64, 512), f(4, 64, 512), f(384, 512), f(4, 256, 256),
        v(8, 32, 768), v(8, 32, 768), v(4, 16, 384), v(8, 16, 384), v(4, 16, 384), v(8, 4, 16, 384),
        v(8, 32, 256), v(8, 32, 256), v(32, 256), v(8, 32, 256), v(32, 256), v(8, 32, 256),
        v(144, 256), v(80, 256), v(48, 256), v(144, 256), v(2, 80, 256), v(4, 48, 256),
        f(64, 512), v(128, 256), v(64, 256), v(32, 256),
        v(128, 256), v(2, 64, 256), v(4, 32, 256), v(384, 256), v(384, 256),
        v(128, 256), v(2, 64, 256), v(4, 32, 256), v(128, 256), v(2, 64, 256), v(4, 32, 256),
        v(128, 256), v(2, 64, 256), v(4, 32, 256), v(128, 256), v(2, 64, 256), v(4, 32, 256),
        v(8, 16, 256), v(8, 16, 256),
        dma((14,)), dma((2, 3, 4)), dma((2, 3, 4)),
        dma((7,)), dma((7,)), dma((7,)), dma((7,)),
        dma((4,)), dma((2, 4)), dma((2, 4)), dma((4,)),
    ] + [dma((2, 7))] * 8 + [dma((7,))] * 6
    out_shape = [pltpu.VMEM(tiles, BF)] * 4 + [pltpu.VMEM((256, 1024), F32)]
    output, gq, gk, gv, wg = pl.pallas_call(
        kernel,
        out_shape=out_shape,
        in_specs=[pl.BlockSpec(memory_space=pltpu.HBM)] * 5,
        out_specs=[pl.BlockSpec(memory_space=pltpu.VMEM)] * 5,
        scratch_shapes=scratch,
        compiler_params=pltpu.CompilerParams(
            collective_id=0, has_side_effects=True, vmem_limit_bytes=48 * 1024 * 1024
        ),
    )(*[
        pltpu.with_memory_space_constraint(a, pltpu.HBM)
        for a in (
            queries.reshape(tiles), keys.reshape(tiles), values.reshape(tiles), out_weight,
            cotangent.reshape(tiles),
        )
    ])
    output, gq, gk, gv, wg = hand_over(output, gq, gk, gv, wg)
    rows = queries.shape
    return output.reshape(rows), gq.reshape(rows), gk.reshape(rows), gv.reshape(rows), wg


def solution(mesh):
    in_specs = (P("tile", "head"), P("tile", "head"), P("tile", "head"), P(), P("tile", "head"))
    out_specs = (
        P("tile", "head"),
        P("tile", "head"),
        P("tile", "head"),
        P("tile", "head"),
        P("head", None),
    )
    return jax.shard_map(local, mesh=mesh, in_specs=in_specs, out_specs=out_specs, check_vma=False)
```

```python
import math

import jax
import jax.numpy as jnp
from jax import lax
from jax.experimental import pallas as pl
from jax.experimental.pallas import tpu as pltpu
from jax.sharding import PartitionSpec as P

BF = jnp.bfloat16
F32 = jnp.float32
MESH = pl.DeviceIdType.MESH
ROOT_HALF = 1.0 / math.sqrt(2.0)
NT = (((1,), (1,)), ((), ()))
TILE = 256
W = 256


def mm(a, b):
    return jnp.dot(a, b, preferred_element_type=F32)


def mm_nt(a, b):
    return lax.dot_general(a, b, NT, preferred_element_type=F32)


def iota(shape, axis):
    return lax.broadcasted_iota(jnp.int32, shape, axis)


def ones_where(mask):
    return jnp.where(mask, 1.0, 0.0).astype(BF)


def pool2(x):
    n = x.shape[0]
    pairs = ones_where((iota((n // 2, n), 1) >> 1) == iota((n // 2, n), 0))
    return (mm(pairs, x) * ROOT_HALF).astype(BF)


def repeat_rows(x, times_log2):
    n = x.shape[0]
    big = n << times_log2
    spread = ones_where((iota((big, n), 0) >> times_log2) == iota((big, n), 1))
    high = x.astype(BF)
    low = (x - high.astype(F32)).astype(BF)
    return mm(spread, high) + mm(spread, low)


def spread(x, levels):
    return repeat_rows(x, levels) * ROOT_HALF ** levels


def block(k):
    return pl.ds(pl.multiple_of(k * W, W), W)


def start_far_first(copies):
    for m in (4, 5, 6, 7, 2, 3, 1):
        copies[m - 1].start()


def lanes(a, b):
    return jnp.concatenate([a, b], axis=1)


def stack_kv(x):
    return jnp.concatenate([x[:, :W], x[:, W:]], axis=0)


def unstack_kv(x):
    n = x.shape[0] // 2
    return jnp.concatenate([x[:n], x[n:]], axis=1)


def kernel(
    q_hbm, k_hbm, v_hbm, w_hbm, c_hbm,
    outr, gq_v, gk_v, gv_v, wgo,
    q_v, ks, vs, kst, vst, w_v, cot, scores, pt_v, dst_v, mixt, mixf, mixed, ma, ob,
    qbd, gbd, inv, base, p0, p1, fg, wpart, wsa, wra, ws2a, wr2a, wg3a, wg4a,
    wsb, wrb, ws2b, wr2b, wg3b, wg4b,
    u0, u1, u2, ru0, ru1, ru2, n3f, h0, h1, h2, rh0, rh1, rh2, fk, fv,
    e0, e1, e2, e3, e4, e5, re0, re1, re2, re3, re4, re5, d3s, rd3,
    in_sem, ag_send, ag_recv, up_send, up_recv, uh_send, uh_recv,
    ma_send, ma_recv, ob_send, ob_recv,
    w1_send, w1_recv, w2_send, w2_recv, w3_send, w3_recv, w4_send, w4_recv,
    dl_send, dl_recv, dh_send, dh_recv, d3_send, d3_recv,
):
    pos = lax.axis_index("tile")
    h = lax.axis_index("head")
    i = pos & 7
    g = pos >> 3

    in_cot = [pltpu.make_async_copy(c_hbm.at[c], cot.at[block(c), block(h)], in_sem.at[c]) for c in range(4)]
    in_k = [pltpu.make_async_copy(k_hbm.at[t], ks.at[t, pl.ds(0, TILE)], in_sem.at[4 + t]) for t in range(4)]
    in_v = [pltpu.make_async_copy(v_hbm.at[t], vs.at[t, pl.ds(0, TILE)], in_sem.at[8 + t]) for t in range(4)]
    in_q = pltpu.make_async_copy(q_hbm, q_v, in_sem.at[12])
    in_w = pltpu.make_async_copy(w_hbm, w_v, in_sem.at[13])
    for copy in in_k + in_v + in_cot + [in_q, in_w]:
        copy.start()

    barrier = pltpu.get_barrier_semaphore()
    for m in (4, 5, 6, 7, 2, 3, 1):
        pl.semaphore_signal(barrier, inc=1, device_id=(pos ^ (8 * m), h), device_id_type=MESH)
    for m in range(1, 4):
        pl.semaphore_signal(barrier, inc=1, device_id=(pos, h ^ m), device_id_type=MESH)
    for m in range(1, 8):
        pl.semaphore_signal(barrier, inc=1, device_id=(pos ^ m, h), device_id_type=MESH)

    def remote(src, dst, send_sem, recv_sem, to_pos, to_head):
        return pltpu.make_async_remote_copy(
            src_ref=src, dst_ref=dst, send_sem=send_sem, recv_sem=recv_sem,
            device_id=(to_pos, to_head), device_id_type=MESH,
        )

    def ag_copy(way, shard, k, c, to_head):
        part = cot.at[block(c), block(shard)]
        return remote(part, part, ag_send.at[way, k, c], ag_recv.at[way, k, c], pos, to_head)

    def ag_right(k, c):
        return ag_copy(0, h - k, k, c, h + 1)

    def ag_left(k, c):
        return ag_copy(1, h + k, k, c, h - 1)

    def ag_wait_right(k, c):
        ag_copy(0, h - k, k - 1, c, h).wait_recv()

    def ag_wait_left(k, c):
        ag_copy(1, h + k, k - 1, c, h).wait_recv()

    def ag_forward(k, c):
        @pl.when(h - k >= 0)
        def _():
            ag_wait_right(k, c)

            @pl.when(h < 3)
            def _():
                ag_right(k, c).start()

        @pl.when(h + k <= 3)
        def _():
            ag_wait_left(k, c)

            @pl.when(h > 0)
            def _():
                ag_left(k, c).start()

    for copy in in_k + in_v:
        copy.wait()
    quads = ones_where((iota((64, TILE), 1) >> 2) == iota((64, TILE), 0))
    leaf = [
        (mm(quads, lanes(ks[t, 0:TILE, :], vs[t, 0:TILE, :])) * 0.5).astype(BF) for t in range(4)
    ]
    node1 = [pool2(jnp.concatenate([leaf[2 * n], leaf[2 * n + 1]], axis=0)) for n in range(2)]
    top = pool2(jnp.concatenate(node1, axis=0))
    pool_1 = pool2(top)
    pool_2 = pool2(pool_1)
    n = 16
    pairs = ones_where((iota((n // 2, n), 1) >> 1) == iota((n // 2, n), 0))
    pool_3f = (mm(pairs, pool_2) * ROOT_HALF).astype(BF).astype(F32)
    pool_3 = jnp.concatenate([pool_3f[:, :W], pool_3f[:, W:]], axis=0).astype(BF)
    u0[0:128, :] = stack_kv(top)
    u0[128:144, :] = pool_3
    u1[0:64, :] = stack_kv(pool_1)
    u1[64:80, :] = pool_3
    u2[0:32, :] = stack_kv(pool_2)
    u2[32:48, :] = pool_3

    for copy in in_cot:
        copy.wait()
    pl.semaphore_wait(barrier, 17)

    def low_pair(m, s0, r0, s1, r1, s2, r2):
        if m == 1:
            return s0, r0
        if m < 4:
            return s1, r1.at[m - 2]
        return s2, r2.at[m - 4]

    up = []
    for m in range(1, 8):
        src, dst = low_pair(m, u0, ru0, u1, ru1, u2, ru2)
        up.append(remote(src, dst, up_send.at[m - 1], up_recv.at[m - 1], pos ^ m, h))
    start_far_first(up)
    for c in range(4):
        @pl.when(h < 3)
        def _():
            ag_right(0, c).start()

        @pl.when(h > 0)
        def _():
            ag_left(0, c).start()


    for t in range(4):
        other = leaf[t ^ 1]
        ks[t, 256:320, :] = other[:, :W]
        vs[t, 256:320, :] = other[:, W:]
        other = node1[(t >> 1) ^ 1]
        ks[t, 320:384, :] = other[:, :W]
        vs[t, 320:384, :] = other[:, W:]
        kst[t, :, 0:384] = ks[t, 0:384, :].T
        vst[t, :, 0:384] = vs[t, 0:384, :].T

    in_q.wait()
    in_w.wait()

    n3f[pl.ds(pl.multiple_of(i * 8, 8), 8), :] = jnp.concatenate([pool_3f[:, :W], pool_3f[:, W:]], axis=1)

    def put_group_part(part, sender):
        part = part.astype(F32)
        n3f[pl.ds(pl.multiple_of(sender * 8, 8), 8), :] = jnp.concatenate([part[0:8], part[8:16]], axis=1)

    for m in range(1, 8):
        up[m - 1].wait_recv()
        sender = i ^ m
        if m == 1:
            fk[0:64, :] = ru0[0:64, :]
            fv[0:64, :] = ru0[64:128, :]
            put_group_part(ru0[128:144, :], sender)
        elif m < 4:
            at = pl.multiple_of(64 + (sender & 1) * 32, 32)
            fk[pl.ds(at, 32), :] = ru1[m - 2, 0:32, :]
            fv[pl.ds(at, 32), :] = ru1[m - 2, 32:64, :]
            put_group_part(ru1[m - 2, 64:80, :], sender)
        else:
            at = pl.multiple_of(128 + (sender & 3) * 16, 16)
            fk[pl.ds(at, 16), :] = ru2[m - 4, 0:16, :]
            fv[pl.ds(at, 16), :] = ru2[m - 4, 16:32, :]
            put_group_part(ru2[m - 4, 32:48, :], sender)
    group_node = n3f[...].astype(BF)
    group_1 = pool2(group_node)
    group_2 = pool2(group_1)
    h0[...] = stack_kv(group_node)
    h1[...] = stack_kv(group_1)
    h2[...] = stack_kv(group_2)
    uh = []
    for m in range(1, 8):
        src, dst = low_pair(m, h0, rh0, h1, rh1, h2, rh2)
        uh.append(remote(src, dst, uh_send.at[m - 1], uh_recv.at[m - 1], pos ^ (8 * m), h))
    start_far_first(uh)

    for c in range(4):
        ag_forward(1, c)

    for m in range(1, 8):
        uh[m - 1].wait_recv()
        sender = g ^ m
        if m == 1:
            fk[192:256, :] = rh0[0:64, :]
            fv[192:256, :] = rh0[64:128, :]
        elif m < 4:
            at = pl.multiple_of(256 + (sender & 1) * 32, 32)
            fk[pl.ds(at, 32), :] = rh1[m - 2, 0:32, :]
            fv[pl.ds(at, 32), :] = rh1[m - 2, 32:64, :]
        else:
            at = pl.multiple_of(320 + (sender & 3) * 16, 16)
            fk[pl.ds(at, 16), :] = rh2[m - 4, 0:16, :]
            fv[pl.ds(at, 16), :] = rh2[m - 4, 16:32, :]
    far_kt = fk[...].T
    far_vt = fv[...].T
    for t in range(4):
        ks[t, 384:768, :] = fk[...]
        vs[t, 384:768, :] = fv[...]
        kst[t, :, 384:768] = far_kt
        vst[t, :, 384:768] = far_vt

    head_masks = [ones_where((iota((TILE, W), 1) >> 6) == hd) for hd in range(4)]

    def send_mixed(t):
        return remote(
            mixed.at[t], ma.at[t & 1, :, block(h)], ma_send.at[t], ma_recv.at[t & 1, h], pos, 1 + (t >> 1)
        )

    middle = jnp.logical_and(h > 0, h < 3)

    def forward(step, carry):
        t = (step + 2 * (1 - (h >> 1))) & 3
        q_tile = q_v[t] * jnp.asarray(0.125, BF)

        def scores_of(hd):
            q_head = q_tile * head_masks[hd]
            peak = None
            for lo in (0, 384):
                part = mm_nt(ks[t, lo:lo + 384, :], q_head)
                scores[hd % 2, lo:lo + 384, :] = part
                part = jnp.max(part.reshape(48, 8, 256), axis=0)
                peak = part if peak is None else jnp.maximum(peak, part)
            return jnp.max(peak, axis=0, keepdims=True)

        def weights_of(hd, peak):
            total = None
            for lo in range(0, 768, 128):
                part = jnp.exp(scores[hd % 2, lo:lo + 128, :] - peak)
                pt_v[t, lo:lo + 128, hd * 256:(hd + 1) * 256] = part.astype(BF)
                part = jnp.sum(part.reshape(16, 8, 256), axis=0)
                total = part if total is None else total + part
            inv[t, hd:hd + 1, :] = 1.0 / jnp.sum(total, axis=0, keepdims=True)

        def mix_of(hd):
            at = slice(hd * 64, (hd + 1) * 64)
            mixf[t, at, :] = mm(vst[t, at, :], pt_v[t, :, hd * 256:(hd + 1) * 256]) * inv[t, hd:hd + 1, :]

        peak = scores_of(0)
        for hd in range(4):
            following = scores_of(hd + 1) if hd < 3 else None
            weights_of(hd, peak)
            peak = following
            if hd > 0:
                mix_of(hd - 1)
        mix_of(3)
        whole = mixf[t]
        mixt[:, block(t)] = whole.astype(BF)
        mixed[t] = whole.T.astype(BF)

        owner = 1 + (t >> 1)

        @pl.when(h != owner)
        def _():
            send_mixed(t).start()

        @pl.when(h == owner)
        def _():
            ma[t & 1, :, block(h)] = mixed[t]

        @pl.when(jnp.logical_and(middle, step > 0))
        def _():
            ag_forward(2, step - 1)

        return carry

    lax.fori_loop(0, 4, forward, 0)

    upper = h >> 1
    order_a = (h, h ^ 1, 2 - upper)
    order_b = (3 * (1 - upper),)

    class Reduction:
        def __init__(self, order, part, bufs):
            self.order, self.part, self.nb = order, part, len(order)
            self.ws, self.wr, self.ws2, self.wr2, self.wg3, self.wg4 = bufs
            self.first = 0 if part == 0 else 3

        def begin(self):
            for j, s in enumerate(self.order):
                part = mm(mixt[...], cot[:, block(s)])
                wpart[self.first + j] = part
                for r in range(8):
                    self.ws[r, :, j * W:(j + 1) * W] = part[r * 32:(r + 1) * 32].astype(BF)
            start_far_first(self.low())

        def low(self):
            return [
                remote(self.ws.at[i ^ m], self.wr.at[m], w1_send.at[self.part, m - 1], w1_recv.at[self.part, m - 1], pos ^ m, h)
                for m in range(1, 8)
            ]

        def high(self):
            return [
                remote(self.ws2.at[(g ^ m) & 3], self.wr2.at[g], w2_send.at[self.part, m - 1], w2_recv.at[self.part, m - 1],
                       pos ^ (8 * m), h)
                for m in range(1, 8)
            ]

        def back_x(self):
            return [
                remote(self.wg3.at[g & 3], self.wg3.at[g & 3], w3_send.at[self.part, m - 1], w3_recv.at[self.part, m - 1],
                       pos ^ (8 * m), h)
                for m in range(1, 4)
            ]

        def back_low(self):
            return [
                remote(self.wg3, self.wg4.at[m], w4_send.at[self.part, m - 1], w4_recv.at[self.part, m - 1], pos ^ m, h)
                for m in range(1, 8)
            ]

        def to_high(self):
            for copy in self.low():
                copy.wait_recv()
            half = self.nb * 128
            rows = pl.ds(pl.multiple_of(i * 32, 32), 32)
            total = jnp.concatenate([wpart[self.first + j, rows, :] for j in range(self.nb)], axis=1)
            for m in range(1, 8):
                total = total + self.wr[m].astype(F32)
            for r in range(4):
                piece = total[r * 8:(r + 1) * 8]
                self.ws2[r] = jnp.concatenate([piece[:, :half], piece[:, half:]], axis=0).astype(BF)
            start_far_first(self.high())
            self.wr2[g] = self.ws2[g & 3]

        def to_back_x(self):
            for m in range(1, 8):
                remote(self.ws2.at[0], self.wr2.at[g ^ m], w2_send.at[self.part, m - 1], w2_recv.at[self.part, m - 1], pos, h).wait_recv()
            total = self.wr2[0].astype(F32)
            for r in range(1, 8):
                total = total + self.wr2[r].astype(F32)
            self.wg3[g & 3] = total.astype(BF)
            for copy in self.back_x():
                copy.start()

        def to_back_low(self):
            for m in range(1, 4):
                slot = self.wg3.at[(g ^ m) & 3]
                remote(slot, slot, w3_send.at[self.part, m - 1], w3_recv.at[self.part, m - 1], pos, h).wait_recv()
            start_far_first(self.back_low())
            self.wg4[0] = self.wg3[...]

        def finish(self):
            for copy in self.back_low():
                copy.wait_recv()
            half = self.nb * 128

            def put(m, carry):
                for r in range(4):
                    rows = pl.ds(pl.multiple_of((i ^ m) * 32 + r * 8, 8), 8)
                    piece = self.wg4[m, r].astype(F32)
                    for c in range(2 * self.nb):
                        top, lane = (c * 128) // half, (c * 128) % half
                        columns = pl.ds(pl.multiple_of(self.order[c // 2] * W + (c % 2) * 128, 128), 128)
                        wgo[rows, columns] = piece[top * 8:(top + 1) * 8, lane:lane + 128]
                return carry

            lax.fori_loop(0, 8, put, 0)

        def wait_sends(self):
            for copy in self.low() + self.high() + self.back_x():
                copy.wait_send()

        def wait_back(self):
            for copy in self.back_low():
                copy.wait_send()

    class Last(Reduction):
        def high(self):
            return [
                remote(self.ws2, self.wr2.at[g], w2_send.at[self.part, m - 1], w2_recv.at[self.part, m - 1], pos ^ (8 * m), h)
                for m in range(1, 8)
            ]

        def to_high(self):
            for copy in self.low():
                copy.wait_recv()
            total = wpart[self.first, pl.ds(pl.multiple_of(i * 32, 32), 32), :]
            for m in range(1, 8):
                total = total + self.wr[m].astype(F32)
            self.ws2[...] = total.astype(BF)
            start_far_first(self.high())
            self.wr2[g] = self.ws2[...]

        def to_back_low(self):
            for m in range(1, 8):
                remote(self.ws2, self.wr2.at[g ^ m], w2_send.at[self.part, m - 1], w2_recv.at[self.part, m - 1], pos, h).wait_recv()
            total = self.wr2[0].astype(F32)
            for r in range(1, 8):
                total = total + self.wr2[r].astype(F32)
            self.wg3[...] = total.astype(BF)
            start_far_first(self.back_low())
            self.wg4[0] = self.wg3[...]

        def finish(self):
            for copy in self.back_low():
                copy.wait_recv()
            for m in range(8):
                wgo[pl.ds(pl.multiple_of((i ^ m) * 32, 32), 32), block(self.order[0])] = self.wg4[m].astype(F32)

        def wait_sends(self):
            for copy in self.low() + self.high():
                copy.wait_send()

    part_a = Reduction(order_a, 0, (wsa, wra, ws2a, wr2a, wg3a, wg4a))
    part_b = Last(order_b, 1, (wsb, wrb, ws2b, wr2b, wg3b, wg4b))

    @pl.when(jnp.logical_not(middle))
    def _():
        for c in range(4):
            ag_forward(2, c)

    part_a.begin()

    @pl.when(middle)
    def _():
        ag_forward(2, 3)

    def send_output(tile, c):
        return remote(ob.at[tile, c], outr.at[2 * (h - 1) + tile], ob_send.at[tile, c], ob_recv.at[2 * (h - 1) + tile], pos, c)

    def send_tile(tile):
        for m in (2, 3, 1):
            send_output(tile, h ^ m).start()

    def project():
        for tile in range(2):
            for s in range(4):
                @pl.when(h != s)
                def _():
                    part = ma.at[tile, :, block(s)]
                    remote(part, part, ma_send.at[0], ma_recv.at[tile, s], pos, h).wait_recv()
        for tile in range(2):
            for c in range(4):
                ob[tile, c] = mm(ma[tile], w_v[:, c * W:(c + 1) * W]).astype(BF)
        for tile in range(2):
            outr[2 * (h - 1) + tile] = ob[tile, h]
        send_tile(0)

    fg[...] = jnp.zeros_like(fg)

    def backward(t, carry):
        @pl.when(h == 3)
        def _():
            ag_wait_right(3, t)

        @pl.when(h == 0)
        def _():
            ag_wait_left(3, t)

        gmt = mm_nt(w_v[block(h), :], cot[block(t), :])
        gmt = jnp.concatenate(
            [gmt[hd * 64:(hd + 1) * 64] * inv[t, hd:hd + 1, :] for hd in range(4)], axis=0
        )
        @pl.when(t == 3 * (1 - (((h + 1) >> 1) & 1)))
        def _():
            part_b.begin()

        gm = gmt.T.astype(BF)
        gmt = gmt.astype(BF).astype(F32)
        q_tile = q_v[t] * jnp.asarray(0.125, BF)
        for hd in range(4):
            part = slice(hd * 256, (hd + 1) * 256)
            gbd[part, :] = gm * head_masks[hd]
            qbd[part, :] = q_tile * head_masks[hd]
        for hd in range(4):
            at = slice(hd * 64, (hd + 1) * 64)
            part = slice(hd * 256, (hd + 1) * 256)
            centre = jnp.sum(gmt[at] * mixf[t, at, :], axis=0, keepdims=True)
            for lo in range(0, 768, 256):
                rows = slice(lo, lo + 256)
                grad_probs = mm_nt(vs[t, rows, :], gbd[part, :])
                dst_v[rows, part] = (pt_v[t, rows, part].astype(F32) * (grad_probs - centre)).astype(BF)
        dqt = []
        for hd in range(4):
            at = slice(hd * 64, (hd + 1) * 64)
            dqt.append(mm(kst[t, at, :], dst_v[:, hd * 256:(hd + 1) * 256]))
        gq_v[t] = (jnp.concatenate(dqt, axis=0) * 0.125).T.astype(BF)
        dk = mm(dst_v[0:384, :], qbd[...])
        dv = mm(pt_v[t, 0:384, :], gbd[...])
        base[t] = lanes(dk[0:256], dv[0:256])
        p0[t] = lanes(dk[256:320], dv[256:320])
        p1[t] = lanes(dk[320:384], dv[320:384])
        fg[:, :W] += mm(dst_v[384:768, :], qbd[...])
        fg[:, W:] += mm(pt_v[t, 384:768, :], gbd[...])

        @pl.when(t == 2)
        def _():
            part_a.to_high()

            @pl.when(middle)
            def _():
                part_b.to_high()

        return carry

    lax.fori_loop(0, 4, backward, 0)

    def level(b):
        return fg[b * 64:(b + 1) * 64, :]

    def cut(buffer, b, parts):
        rows = 64 // parts
        whole = level(b)
        for part in range(parts):
            buffer[part] = stack_kv(whole[part * rows:(part + 1) * rows]).astype(BF)

    e3[...] = stack_kv(level(3)).astype(BF)
    cut(e4, 4, 2)
    cut(e5, 5, 4)

    def down_pair(m, index, s0, r0, s1, r1, s2, r2):
        if m == 1:
            return s0, r0
        if m < 4:
            return s1.at[(index ^ m) & 1], r1.at[m - 2]
        return s2.at[(index ^ m) & 3], r2.at[m - 4]

    dh = []
    for m in range(1, 8):
        src, dst = down_pair(m, g, e3, re3, e4, re4, e5, re5)
        dh.append(remote(src, dst, dh_send.at[m - 1], dh_recv.at[m - 1], pos ^ (8 * m), h))
    start_far_first(dh)
    @pl.when(middle)
    def _():
        project()

    @pl.when(jnp.logical_not(middle))
    def _():
        part_b.to_high()

    part_a.to_back_x()
    e0[...] = stack_kv(level(0)).astype(BF)
    cut(e1, 1, 2)
    cut(e2, 2, 4)
    dl = []
    for m in range(1, 8):
        src, dst = down_pair(m, i, e0, re0, e1, re1, e2, re2)
        dl.append(remote(src, dst, dl_send.at[m - 1], dl_recv.at[m - 1], pos ^ m, h))
    start_far_first(dl)


    part_a.to_back_low()

    def f32_kv(x):
        return unstack_kv(x.astype(F32))

    def total_of(buffer, count):
        total = f32_kv(buffer[0])
        for k in range(1, count):
            total = total + f32_kv(buffer[k])
        return total

    for copy in up + uh:
        copy.wait_send()
    for t in range(4):
        @pl.when(h != 1 + (t >> 1))
        def _():
            send_mixed(t).wait_send()
    for k in range(3):
        for c in range(4):
            @pl.when(jnp.logical_and(h - k >= 0, h < 3))
            def _():
                ag_right(k, c).wait_send()

            @pl.when(jnp.logical_and(h + k <= 3, h > 0))
            def _():
                ag_left(k, c).wait_send()

    for copy in dh:
        copy.wait_recv()

    group_grad = f32_kv(re3[...]) + spread(total_of(re4, 2), 1) + spread(total_of(re5, 4), 2)
    for r in range(8):
        d3s[r] = stack_kv(group_grad[r * 8:(r + 1) * 8]).astype(BF)
    d3 = []
    for m in range(1, 8):
        d3.append(remote(d3s.at[i ^ m], rd3.at[m], d3_send.at[m - 1], d3_recv.at[m - 1], pos ^ m, h))
    start_far_first(d3)

    part_b.to_back_low()

    @pl.when(middle)
    def _():
        send_tile(1)

    for copy in dl:
        copy.wait_recv()
    top_grad = f32_kv(re0[...]) + spread(total_of(re1, 2), 1) + spread(total_of(re2, 4), 2)
    for n in range(2):
        first = 2 * (1 - n)
        down_1 = p1[first] + p1[first + 1] + spread(top_grad[n * 32:(n + 1) * 32], 1)
        for r in range(2):
            t = 2 * n + r
            down_0 = p0[t ^ 1] + spread(down_1[r * 32:(r + 1) * 32], 1)
            base[t] += repeat_rows(down_0, 2) * 0.5

    for copy in dl + dh:
        copy.wait_send()
    part_a.wait_sends()
    part_b.wait_sends()
    for copy in d3:
        copy.wait_recv()
    eighth = f32_kv(d3s[i])
    for m in range(1, 8):
        eighth = eighth + f32_kv(rd3[m])
    eighth = eighth * (0.25 * ROOT_HALF ** 3)
    for t in range(4):
        for half in range(2):
            rows = slice(half * 128, (half + 1) * 128)
            whole = base[t, rows, :] + eighth[2 * t + half:2 * t + half + 1, :]
            gk_v[t, rows, :] = whole[:, :W].astype(BF)
            gv_v[t, rows, :] = whole[:, W:].astype(BF)
    part_a.finish()
    for t in range(4):
        @pl.when(h != 1 + (t >> 1))
        def _():
            remote(outr.at[t], outr.at[t], ob_send.at[0, 0], ob_recv.at[t], pos, h).wait_recv()
    part_b.finish()

    for copy in d3:
        copy.wait_send()
    part_a.wait_back()
    part_b.wait_back()
    for tile in range(2):
        for c in range(4):
            @pl.when(jnp.logical_and(middle, h != c))
            def _():
                send_output(tile, c).wait_send()


def hand_over(*arrays):
    n = len(arrays)

    def copy_kernel(*refs):
        sems = refs[2 * n]
        copies = []
        for k in range(n):
            size = arrays[k].shape[0] // 4
            for part in range(4):
                cut = pl.ds(part * size, size)
                copies.append(pltpu.make_async_copy(refs[k].at[cut], refs[n + k].at[cut], sems.at[k, part]))
        for copy in copies:
            copy.start()
        for copy in copies:
            copy.wait()

    return pl.pallas_call(
        copy_kernel,
        out_shape=[jax.ShapeDtypeStruct(a.shape, a.dtype) for a in arrays],
        in_specs=[pl.BlockSpec(memory_space=pltpu.VMEM)] * n,
        out_specs=[pl.BlockSpec(memory_space=pltpu.HBM)] * n,
        scratch_shapes=[pltpu.SemaphoreType.DMA((n, 4))],
    )(*[pltpu.with_memory_space_constraint(a, pltpu.VMEM) for a in arrays])


def local(queries, keys, values, out_weight, cotangent):
    tiles = (4, TILE, W)

    def v(*shape, dtype=BF):
        return pltpu.VMEM(shape, dtype)

    def f(*shape):
        return pltpu.VMEM(shape, F32)

    dma = pltpu.SemaphoreType.DMA
    scratch = [
        v(4, 256, 256), v(4, 768, 256), v(4, 768, 256), v(4, 256, 768), v(4, 256, 768),
        v(1024, 1024), v(1024, 1024), f(2, 768, 256), v(4, 768, 1024), v(768, 1024),
        v(256, 1024), f(4, 256, 256), v(4, 256, 256), v(2, 256, 1024),
        v(2, 4, 256, 256),
        v(1024, 256), v(1024, 256), f(4, 8, 256), f(4, 256, 512),
        f(4, 64, 512), f(4, 64, 512), f(384, 512), f(4, 256, 256),
        v(8, 32, 768), v(8, 32, 768), v(4, 16, 384), v(8, 16, 384), v(4, 16, 384), v(8, 4, 16, 384),
        v(8, 32, 256), v(8, 32, 256), v(32, 256), v(8, 32, 256), v(32, 256), v(8, 32, 256),
        v(144, 256), v(80, 256), v(48, 256), v(144, 256), v(2, 80, 256), v(4, 48, 256),
        f(64, 512), v(128, 256), v(64, 256), v(32, 256),
        v(128, 256), v(2, 64, 256), v(4, 32, 256), v(384, 256), v(384, 256),
        v(128, 256), v(2, 64, 256), v(4, 32, 256), v(128, 256), v(2, 64, 256), v(4, 32, 256),
        v(128, 256), v(2, 64, 256), v(4, 32, 256), v(128, 256), v(2, 64, 256), v(4, 32, 256),
        v(8, 16, 256), v(8, 16, 256),
        dma((14,)), dma((2, 3, 4)), dma((2, 3, 4)),
        dma((7,)), dma((7,)), dma((7,)), dma((7,)),
        dma((4,)), dma((2, 4)), dma((2, 4)), dma((4,)),
    ] + [dma((2, 7))] * 8 + [dma((7,))] * 6
    out_shape = [pltpu.VMEM(tiles, BF)] * 4 + [pltpu.VMEM((256, 1024), F32)]
    output, gq, gk, gv, wg = pl.pallas_call(
        kernel,
        out_shape=out_shape,
        in_specs=[pl.BlockSpec(memory_space=pltpu.HBM)] * 5,
        out_specs=[pl.BlockSpec(memory_space=pltpu.VMEM)] * 5,
        scratch_shapes=scratch,
        compiler_params=pltpu.CompilerParams(
            collective_id=0, has_side_effects=True, vmem_limit_bytes=48 * 1024 * 1024
        ),
    )(*[
        pltpu.with_memory_space_constraint(a, pltpu.HBM)
        for a in (
            queries.reshape(tiles), keys.reshape(tiles), values.reshape(tiles), out_weight,
            cotangent.reshape(tiles),
        )
    ])
    output, gq, gk, gv, wg = hand_over(output, gq, gk, gv, wg)
    rows = queries.shape
    return output.reshape(rows), gq.reshape(rows), gk.reshape(rows), gv.reshape(rows), wg


def solution(mesh):
    in_specs = (P("tile", "head"), P("tile", "head"), P("tile", "head"), P(), P("tile", "head"))
    out_specs = (
        P("tile", "head"),
        P("tile", "head"),
        P("tile", "head"),
        P("tile", "head"),
        P("head", None),
    )
    return jax.shard_map(local, mesh=mesh, in_specs=in_specs, out_specs=out_specs, check_vma=False)
```

```python
import math

import jax
import jax.numpy as jnp
from jax import lax
from jax.experimental import pallas as pl
from jax.experimental.pallas import tpu as pltpu
from jax.sharding import PartitionSpec as P

BF = jnp.bfloat16
F32 = jnp.float32
MESH = pl.DeviceIdType.MESH
ROOT_HALF = 1.0 / math.sqrt(2.0)
NT = (((1,), (1,)), ((), ()))
TILE = 256
W = 256


def mm(a, b):
    return jnp.dot(a, b, preferred_element_type=F32)


def mm_nt(a, b):
    return lax.dot_general(a, b, NT, preferred_element_type=F32)


def iota(shape, axis):
    return lax.broadcasted_iota(jnp.int32, shape, axis)


def ones_where(mask):
    return jnp.where(mask, 1.0, 0.0).astype(BF)


def pool2(x):
    n = x.shape[0]
    pairs = ones_where((iota((n // 2, n), 1) >> 1) == iota((n // 2, n), 0))
    return (mm(pairs, x) * ROOT_HALF).astype(BF)


def repeat_rows(x, times_log2):
    n = x.shape[0]
    big = n << times_log2
    spread = ones_where((iota((big, n), 0) >> times_log2) == iota((big, n), 1))
    high = x.astype(BF)
    low = (x - high.astype(F32)).astype(BF)
    return mm(spread, high) + mm(spread, low)


def spread(x, levels):
    return repeat_rows(x, levels) * ROOT_HALF ** levels


def block(k):
    return pl.ds(pl.multiple_of(k * W, W), W)


def start_far_first(copies):
    for m in (4, 5, 6, 7, 2, 3, 1):
        copies[m - 1].start()


def lanes(a, b):
    return jnp.concatenate([a, b], axis=1)


def stack_kv(x):
    return jnp.concatenate([x[:, :W], x[:, W:]], axis=0)


def unstack_kv(x):
    n = x.shape[0] // 2
    return jnp.concatenate([x[:n], x[n:]], axis=1)


def kernel(
    q_hbm, k_hbm, v_hbm, w_hbm, c_hbm,
    outr, gq_v, gk_v, gv_v, wgo,
    q_v, ks, vs, kst, vst, w_v, cot, scores, pt_v, dst_v, mixt, mixf, mixed, ma, ob,
    qbd, gbd, inv, base, p0, p1, fg, wpart, wsa, wra, ws2a, wr2a, wg3a, wg4a,
    wsb, wrb, ws2b, wr2b, wg3b, wg4b,
    u0, u1, u2, ru0, ru1, ru2, n3f, h0, h1, h2, rh0, rh1, rh2, fk, fv,
    e0, e1, e2, e3, e4, e5, re0, re1, re2, re3, re4, re5, d3s, rd3,
    in_sem, ag_send, ag_recv, up_send, up_recv, uh_send, uh_recv,
    ma_send, ma_recv, ob_send, ob_recv,
    w1_send, w1_recv, w2_send, w2_recv, w3_send, w3_recv, w4_send, w4_recv,
    dl_send, dl_recv, dh_send, dh_recv, d3_send, d3_recv,
):
    pos = lax.axis_index("tile")
    h = lax.axis_index("head")
    i = pos & 7
    g = pos >> 3

    in_cot = [pltpu.make_async_copy(c_hbm.at[c], cot.at[block(c), block(h)], in_sem.at[c]) for c in range(4)]
    in_k = [pltpu.make_async_copy(k_hbm.at[t], ks.at[t, pl.ds(0, TILE)], in_sem.at[4 + t]) for t in range(4)]
    in_v = [pltpu.make_async_copy(v_hbm.at[t], vs.at[t, pl.ds(0, TILE)], in_sem.at[8 + t]) for t in range(4)]
    in_q = pltpu.make_async_copy(q_hbm, q_v, in_sem.at[12])
    in_w = pltpu.make_async_copy(w_hbm, w_v, in_sem.at[13])
    for copy in in_k + in_v + in_cot + [in_q, in_w]:
        copy.start()

    barrier = pltpu.get_barrier_semaphore()
    for m in (4, 5, 6, 7, 2, 3, 1):
        pl.semaphore_signal(barrier, inc=1, device_id=(pos ^ (8 * m), h), device_id_type=MESH)
    for m in range(1, 4):
        pl.semaphore_signal(barrier, inc=1, device_id=(pos, h ^ m), device_id_type=MESH)
    for m in range(1, 8):
        pl.semaphore_signal(barrier, inc=1, device_id=(pos ^ m, h), device_id_type=MESH)

    def remote(src, dst, send_sem, recv_sem, to_pos, to_head):
        return pltpu.make_async_remote_copy(
            src_ref=src, dst_ref=dst, send_sem=send_sem, recv_sem=recv_sem,
            device_id=(to_pos, to_head), device_id_type=MESH,
        )

    def ag_copy(way, shard, k, c, to_head):
        part = cot.at[block(c), block(shard)]
        return remote(part, part, ag_send.at[way, k, c], ag_recv.at[way, k, c], pos, to_head)

    def ag_right(k, c):
        return ag_copy(0, h - k, k, c, h + 1)

    def ag_left(k, c):
        return ag_copy(1, h + k, k, c, h - 1)

    def ag_wait_right(k, c):
        ag_copy(0, h - k, k - 1, c, h).wait_recv()

    def ag_wait_left(k, c):
        ag_copy(1, h + k, k - 1, c, h).wait_recv()

    def ag_forward(k, c):
        @pl.when(h - k >= 0)
        def _():
            ag_wait_right(k, c)

            @pl.when(h < 3)
            def _():
                ag_right(k, c).start()

        @pl.when(h + k <= 3)
        def _():
            ag_wait_left(k, c)

            @pl.when(h > 0)
            def _():
                ag_left(k, c).start()

    for copy in in_k + in_v:
        copy.wait()
    quads = ones_where((iota((64, TILE), 1) >> 2) == iota((64, TILE), 0))
    leaf = [
        (mm(quads, lanes(ks[t, 0:TILE, :], vs[t, 0:TILE, :])) * 0.5).astype(BF) for t in range(4)
    ]
    node1 = [pool2(jnp.concatenate([leaf[2 * n], leaf[2 * n + 1]], axis=0)) for n in range(2)]
    top = pool2(jnp.concatenate(node1, axis=0))
    pool_1 = pool2(top)
    pool_2 = pool2(pool_1)
    n = 16
    pairs = ones_where((iota((n // 2, n), 1) >> 1) == iota((n // 2, n), 0))
    pool_3f = (mm(pairs, pool_2) * ROOT_HALF).astype(BF).astype(F32)
    pool_3 = jnp.concatenate([pool_3f[:, :W], pool_3f[:, W:]], axis=0).astype(BF)
    u0[0:128, :] = stack_kv(top)
    u0[128:144, :] = pool_3
    u1[0:64, :] = stack_kv(pool_1)
    u1[64:80, :] = pool_3
    u2[0:32, :] = stack_kv(pool_2)
    u2[32:48, :] = pool_3

    for copy in in_cot:
        copy.wait()
    pl.semaphore_wait(barrier, 17)

    def low_pair(m, s0, r0, s1, r1, s2, r2):
        if m == 1:
            return s0, r0
        if m < 4:
            return s1, r1.at[m - 2]
        return s2, r2.at[m - 4]

    up = []
    for m in range(1, 8):
        src, dst = low_pair(m, u0, ru0, u1, ru1, u2, ru2)
        up.append(remote(src, dst, up_send.at[m - 1], up_recv.at[m - 1], pos ^ m, h))
    start_far_first(up)
    for c in range(4):
        @pl.when(h < 3)
        def _():
            ag_right(0, c).start()

        @pl.when(h > 0)
        def _():
            ag_left(0, c).start()


    for t in range(4):
        other = leaf[t ^ 1]
        ks[t, 256:320, :] = other[:, :W]
        vs[t, 256:320, :] = other[:, W:]
        other = node1[(t >> 1) ^ 1]
        ks[t, 320:384, :] = other[:, :W]
        vs[t, 320:384, :] = other[:, W:]
        kst[t, :, 0:384] = ks[t, 0:384, :].T
        vst[t, :, 0:384] = vs[t, 0:384, :].T

    in_q.wait()
    in_w.wait()

    n3f[pl.ds(pl.multiple_of(i * 8, 8), 8), :] = jnp.concatenate([pool_3f[:, :W], pool_3f[:, W:]], axis=1)

    def put_group_part(part, sender):
        part = part.astype(F32)
        n3f[pl.ds(pl.multiple_of(sender * 8, 8), 8), :] = jnp.concatenate([part[0:8], part[8:16]], axis=1)

    for m in range(1, 8):
        up[m - 1].wait_recv()
        sender = i ^ m
        if m == 1:
            fk[0:64, :] = ru0[0:64, :]
            fv[0:64, :] = ru0[64:128, :]
            put_group_part(ru0[128:144, :], sender)
        elif m < 4:
            at = pl.multiple_of(64 + (sender & 1) * 32, 32)
            fk[pl.ds(at, 32), :] = ru1[m - 2, 0:32, :]
            fv[pl.ds(at, 32), :] = ru1[m - 2, 32:64, :]
            put_group_part(ru1[m - 2, 64:80, :], sender)
        else:
            at = pl.multiple_of(128 + (sender & 3) * 16, 16)
            fk[pl.ds(at, 16), :] = ru2[m - 4, 0:16, :]
            fv[pl.ds(at, 16), :] = ru2[m - 4, 16:32, :]
            put_group_part(ru2[m - 4, 32:48, :], sender)
    group_node = n3f[...].astype(BF)
    group_1 = pool2(group_node)
    group_2 = pool2(group_1)
    h0[...] = stack_kv(group_node)
    h1[...] = stack_kv(group_1)
    h2[...] = stack_kv(group_2)
    uh = []
    for m in range(1, 8):
        src, dst = low_pair(m, h0, rh0, h1, rh1, h2, rh2)
        uh.append(remote(src, dst, uh_send.at[m - 1], uh_recv.at[m - 1], pos ^ (8 * m), h))
    start_far_first(uh)

    for c in range(4):
        ag_forward(1, c)

    for m in range(1, 8):
        uh[m - 1].wait_recv()
        sender = g ^ m
        if m == 1:
            fk[192:256, :] = rh0[0:64, :]
            fv[192:256, :] = rh0[64:128, :]
        elif m < 4:
            at = pl.multiple_of(256 + (sender & 1) * 32, 32)
            fk[pl.ds(at, 32), :] = rh1[m - 2, 0:32, :]
            fv[pl.ds(at, 32), :] = rh1[m - 2, 32:64, :]
        else:
            at = pl.multiple_of(320 + (sender & 3) * 16, 16)
            fk[pl.ds(at, 16), :] = rh2[m - 4, 0:16, :]
            fv[pl.ds(at, 16), :] = rh2[m - 4, 16:32, :]
    far_kt = fk[...].T
    far_vt = fv[...].T
    for t in range(4):
        ks[t, 384:768, :] = fk[...]
        vs[t, 384:768, :] = fv[...]
        kst[t, :, 384:768] = far_kt
        vst[t, :, 384:768] = far_vt

    head_masks = [ones_where((iota((TILE, W), 1) >> 6) == hd) for hd in range(4)]

    def send_mixed(t):
        return remote(
            mixed.at[t], ma.at[t & 1, :, block(h)], ma_send.at[t], ma_recv.at[t & 1, h], pos, 1 + (t >> 1)
        )

    middle = jnp.logical_and(h > 0, h < 3)

    def forward(step, carry):
        t = (step + 2 * (1 - (h >> 1))) & 3
        q_tile = q_v[t] * jnp.asarray(0.125, BF)

        def scores_of(hd):
            q_head = q_tile * head_masks[hd]
            peak = None
            for lo in (0, 384):
                part = mm_nt(ks[t, lo:lo + 384, :], q_head)
                scores[hd % 2, lo:lo + 384, :] = part
                part = jnp.max(part.reshape(48, 8, 256), axis=0)
                peak = part if peak is None else jnp.maximum(peak, part)
            return jnp.max(peak, axis=0, keepdims=True)

        def weights_of(hd, peak):
            total = None
            for lo in range(0, 768, 128):
                part = jnp.exp(scores[hd % 2, lo:lo + 128, :] - peak)
                pt_v[t, lo:lo + 128, hd * 256:(hd + 1) * 256] = part.astype(BF)
                part = jnp.sum(part.reshape(16, 8, 256), axis=0)
                total = part if total is None else total + part
            inv[t, hd:hd + 1, :] = 1.0 / jnp.sum(total, axis=0, keepdims=True)

        def mix_of(hd):
            at = slice(hd * 64, (hd + 1) * 64)
            mixf[t, at, :] = mm(vst[t, at, :], pt_v[t, :, hd * 256:(hd + 1) * 256]) * inv[t, hd:hd + 1, :]

        peak = scores_of(0)
        for hd in range(4):
            following = scores_of(hd + 1) if hd < 3 else None
            weights_of(hd, peak)
            peak = following
            if hd > 0:
                mix_of(hd - 1)
        mix_of(3)
        whole = mixf[t]
        mixt[:, block(t)] = whole.astype(BF)
        mixed[t] = whole.T.astype(BF)

        owner = 1 + (t >> 1)

        @pl.when(h != owner)
        def _():
            send_mixed(t).start()

        @pl.when(h == owner)
        def _():
            ma[t & 1, :, block(h)] = mixed[t]

        @pl.when(jnp.logical_and(middle, step > 0))
        def _():
            ag_forward(2, step - 1)

        return carry

    lax.fori_loop(0, 4, forward, 0)

    upper = h >> 1
    order_a = (h, h ^ 1, 2 - upper)
    order_b = (3 * (1 - upper),)

    class Reduction:
        def __init__(self, order, part, bufs):
            self.order, self.part, self.nb = order, part, len(order)
            self.ws, self.wr, self.ws2, self.wr2, self.wg3, self.wg4 = bufs
            self.first = 0 if part == 0 else 3

        def begin(self):
            for j, s in enumerate(self.order):
                part = mm(mixt[...], cot[:, block(s)])
                wpart[self.first + j] = part
                for r in range(8):
                    self.ws[r, :, j * W:(j + 1) * W] = part[r * 32:(r + 1) * 32].astype(BF)
            start_far_first(self.low())

        def low(self):
            return [
                remote(self.ws.at[i ^ m], self.wr.at[m], w1_send.at[self.part, m - 1], w1_recv.at[self.part, m - 1], pos ^ m, h)
                for m in range(1, 8)
            ]

        def high(self):
            return [
                remote(self.ws2.at[(g ^ m) & 3], self.wr2.at[g], w2_send.at[self.part, m - 1], w2_recv.at[self.part, m - 1],
                       pos ^ (8 * m), h)
                for m in range(1, 8)
            ]

        def back_x(self):
            return [
                remote(self.wg3.at[g & 3], self.wg3.at[g & 3], w3_send.at[self.part, m - 1], w3_recv.at[self.part, m - 1],
                       pos ^ (8 * m), h)
                for m in range(1, 4)
            ]

        def back_low(self):
            return [
                remote(self.wg3, self.wg4.at[m], w4_send.at[self.part, m - 1], w4_recv.at[self.part, m - 1], pos ^ m, h)
                for m in range(1, 8)
            ]

        def to_high(self):
            for copy in self.low():
                copy.wait_recv()
            half = self.nb * 128
            rows = pl.ds(pl.multiple_of(i * 32, 32), 32)
            total = jnp.concatenate([wpart[self.first + j, rows, :] for j in range(self.nb)], axis=1)
            for m in range(1, 8):
                total = total + self.wr[m].astype(F32)
            for r in range(4):
                piece = total[r * 8:(r + 1) * 8]
                self.ws2[r] = jnp.concatenate([piece[:, :half], piece[:, half:]], axis=0).astype(BF)
            start_far_first(self.high())
            self.wr2[g] = self.ws2[g & 3]

        def to_back_x(self):
            for m in range(1, 8):
                remote(self.ws2.at[0], self.wr2.at[g ^ m], w2_send.at[self.part, m - 1], w2_recv.at[self.part, m - 1], pos, h).wait_recv()
            total = self.wr2[0].astype(F32)
            for r in range(1, 8):
                total = total + self.wr2[r].astype(F32)
            self.wg3[g & 3] = total.astype(BF)
            for copy in self.back_x():
                copy.start()

        def to_back_low(self):
            for m in range(1, 4):
                slot = self.wg3.at[(g ^ m) & 3]
                remote(slot, slot, w3_send.at[self.part, m - 1], w3_recv.at[self.part, m - 1], pos, h).wait_recv()
            start_far_first(self.back_low())
            self.wg4[0] = self.wg3[...]

        def finish(self):
            for copy in self.back_low():
                copy.wait_recv()
            half = self.nb * 128

            def put(m, carry):
                for r in range(4):
                    rows = pl.ds(pl.multiple_of((i ^ m) * 32 + r * 8, 8), 8)
                    piece = self.wg4[m, r].astype(F32)
                    for c in range(2 * self.nb):
                        top, lane = (c * 128) // half, (c * 128) % half
                        columns = pl.ds(pl.multiple_of(self.order[c // 2] * W + (c % 2) * 128, 128), 128)
                        wgo[rows, columns] = piece[top * 8:(top + 1) * 8, lane:lane + 128]
                return carry

            lax.fori_loop(0, 8, put, 0)

        def wait_sends(self):
            for copy in self.low() + self.high() + self.back_x():
                copy.wait_send()

        def wait_back(self):
            for copy in self.back_low():
                copy.wait_send()

    class Last(Reduction):
        def high(self):
            return [
                remote(self.ws2, self.wr2.at[g], w2_send.at[self.part, m - 1], w2_recv.at[self.part, m - 1], pos ^ (8 * m), h)
                for m in range(1, 8)
            ]

        def to_high(self):
            for copy in self.low():
                copy.wait_recv()
            total = wpart[self.first, pl.ds(pl.multiple_of(i * 32, 32), 32), :]
            for m in range(1, 8):
                total = total + self.wr[m].astype(F32)
            self.ws2[...] = total.astype(BF)
            start_far_first(self.high())
            self.wr2[g] = self.ws2[...]

        def to_back_low(self):
            for m in range(1, 8):
                remote(self.ws2, self.wr2.at[g ^ m], w2_send.at[self.part, m - 1], w2_recv.at[self.part, m - 1], pos, h).wait_recv()
            total = self.wr2[0].astype(F32)
            for r in range(1, 8):
                total = total + self.wr2[r].astype(F32)
            self.wg3[...] = total.astype(BF)
            start_far_first(self.back_low())
            self.wg4[0] = self.wg3[...]

        def finish(self):
            for copy in self.back_low():
                copy.wait_recv()
            for m in range(8):
                wgo[pl.ds(pl.multiple_of((i ^ m) * 32, 32), 32), block(self.order[0])] = self.wg4[m].astype(F32)

        def wait_sends(self):
            for copy in self.low() + self.high():
                copy.wait_send()

    part_a = Reduction(order_a, 0, (wsa, wra, ws2a, wr2a, wg3a, wg4a))
    part_b = Last(order_b, 1, (wsb, wrb, ws2b, wr2b, wg3b, wg4b))

    @pl.when(jnp.logical_not(middle))
    def _():
        for c in range(4):
            ag_forward(2, c)

    part_a.begin()

    @pl.when(middle)
    def _():
        ag_forward(2, 3)

    def send_output(tile, c):
        return remote(ob.at[tile, c], outr.at[2 * (h - 1) + tile], ob_send.at[tile, c], ob_recv.at[2 * (h - 1) + tile], pos, c)

    def send_tile(tile):
        for m in (2, 3, 1):
            send_output(tile, h ^ m).start()

    def project():
        for tile in range(2):
            for s in range(4):
                @pl.when(h != s)
                def _():
                    part = ma.at[tile, :, block(s)]
                    remote(part, part, ma_send.at[0], ma_recv.at[tile, s], pos, h).wait_recv()
        for tile in range(2):
            for c in range(4):
                ob[tile, c] = mm(ma[tile], w_v[:, c * W:(c + 1) * W]).astype(BF)
        for tile in range(2):
            outr[2 * (h - 1) + tile] = ob[tile, h]
        send_tile(0)

    fg[...] = jnp.zeros_like(fg)

    def backward(t, carry):
        @pl.when(h == 3)
        def _():
            ag_wait_right(3, t)

        @pl.when(h == 0)
        def _():
            ag_wait_left(3, t)

        gmt = mm_nt(w_v[block(h), :], cot[block(t), :])
        gmt = jnp.concatenate(
            [gmt[hd * 64:(hd + 1) * 64] * inv[t, hd:hd + 1, :] for hd in range(4)], axis=0
        )
        @pl.when(t == 3 * (1 - (((h + 1) >> 1) & 1)))
        def _():
            part_b.begin()

        gm = gmt.T.astype(BF)
        gmt = gmt.astype(BF).astype(F32)
        q_tile = q_v[t] * jnp.asarray(0.125, BF)
        for hd in range(4):
            part = slice(hd * 256, (hd + 1) * 256)
            gbd[part, :] = gm * head_masks[hd]
            qbd[part, :] = q_tile * head_masks[hd]
        for hd in range(4):
            at = slice(hd * 64, (hd + 1) * 64)
            part = slice(hd * 256, (hd + 1) * 256)
            centre = jnp.sum(gmt[at] * mixf[t, at, :], axis=0, keepdims=True)
            for lo in range(0, 768, 256):
                rows = slice(lo, lo + 256)
                grad_probs = mm_nt(vs[t, rows, :], gbd[part, :])
                dst_v[rows, part] = (pt_v[t, rows, part].astype(F32) * (grad_probs - centre)).astype(BF)
        dqt = []
        for hd in range(4):
            at = slice(hd * 64, (hd + 1) * 64)
            dqt.append(mm(kst[t, at, :], dst_v[:, hd * 256:(hd + 1) * 256]))
        gq_v[t] = (jnp.concatenate(dqt, axis=0) * 0.125).T.astype(BF)
        dk = mm(dst_v[0:384, :], qbd[...])
        dv = mm(pt_v[t, 0:384, :], gbd[...])
        base[t] = lanes(dk[0:256], dv[0:256])
        p0[t] = lanes(dk[256:320], dv[256:320])
        p1[t] = lanes(dk[320:384], dv[320:384])
        fg[:, :W] += mm(dst_v[384:768, :], qbd[...])
        fg[:, W:] += mm(pt_v[t, 384:768, :], gbd[...])

        @pl.when(t == 2)
        def _():
            part_a.to_high()

            @pl.when(middle)
            def _():
                part_b.to_high()

        return carry

    lax.fori_loop(0, 4, backward, 0)

    def level(b):
        return fg[b * 64:(b + 1) * 64, :]

    def cut(buffer, b, parts):
        rows = 64 // parts
        whole = level(b)
        for part in range(parts):
            buffer[part] = stack_kv(whole[part * rows:(part + 1) * rows]).astype(BF)

    e3[...] = stack_kv(level(3)).astype(BF)
    cut(e4, 4, 2)
    cut(e5, 5, 4)

    def down_pair(m, index, s0, r0, s1, r1, s2, r2):
        if m == 1:
            return s0, r0
        if m < 4:
            return s1.at[(index ^ m) & 1], r1.at[m - 2]
        return s2.at[(index ^ m) & 3], r2.at[m - 4]

    dh = []
    for m in range(1, 8):
        src, dst = down_pair(m, g, e3, re3, e4, re4, e5, re5)
        dh.append(remote(src, dst, dh_send.at[m - 1], dh_recv.at[m - 1], pos ^ (8 * m), h))
    start_far_first(dh)
    @pl.when(middle)
    def _():
        project()

    @pl.when(jnp.logical_not(middle))
    def _():
        part_b.to_high()

    part_a.to_back_x()
    e0[...] = stack_kv(level(0)).astype(BF)
    cut(e1, 1, 2)
    cut(e2, 2, 4)
    dl = []
    for m in range(1, 8):
        src, dst = down_pair(m, i, e0, re0, e1, re1, e2, re2)
        dl.append(remote(src, dst, dl_send.at[m - 1], dl_recv.at[m - 1], pos ^ m, h))
    start_far_first(dl)


    part_a.to_back_low()

    def f32_kv(x):
        return unstack_kv(x.astype(F32))

    def total_of(buffer, count):
        total = f32_kv(buffer[0])
        for k in range(1, count):
            total = total + f32_kv(buffer[k])
        return total

    for copy in up + uh:
        copy.wait_send()
    for t in range(4):
        @pl.when(h != 1 + (t >> 1))
        def _():
            send_mixed(t).wait_send()
    for k in range(3):
        for c in range(4):
            @pl.when(jnp.logical_and(h - k >= 0, h < 3))
            def _():
                ag_right(k, c).wait_send()

            @pl.when(jnp.logical_and(h + k <= 3, h > 0))
            def _():
                ag_left(k, c).wait_send()

    for copy in dh:
        copy.wait_recv()

    group_grad = f32_kv(re3[...]) + spread(total_of(re4, 2), 1) + spread(total_of(re5, 4), 2)
    for r in range(8):
        d3s[r] = stack_kv(group_grad[r * 8:(r + 1) * 8]).astype(BF)
    d3 = []
    for m in range(1, 8):
        d3.append(remote(d3s.at[i ^ m], rd3.at[m], d3_send.at[m - 1], d3_recv.at[m - 1], pos ^ m, h))
    start_far_first(d3)

    part_b.to_back_low()

    @pl.when(middle)
    def _():
        send_tile(1)

    for copy in dl:
        copy.wait_recv()
    top_grad = f32_kv(re0[...]) + spread(total_of(re1, 2), 1) + spread(total_of(re2, 4), 2)
    for n in range(2):
        first = 2 * (1 - n)
        down_1 = p1[first] + p1[first + 1] + spread(top_grad[n * 32:(n + 1) * 32], 1)
        for r in range(2):
            t = 2 * n + r
            down_0 = p0[t ^ 1] + spread(down_1[r * 32:(r + 1) * 32], 1)
            base[t] += repeat_rows(down_0, 2) * 0.5

    for copy in dl + dh:
        copy.wait_send()
    part_a.wait_sends()
    part_b.wait_sends()
    part_a.finish()
    for copy in d3:
        copy.wait_recv()
    eighth = f32_kv(d3s[i])
    for m in range(1, 8):
        eighth = eighth + f32_kv(rd3[m])
    eighth = eighth * (0.25 * ROOT_HALF ** 3)
    for t in range(4):
        for half in range(2):
            rows = slice(half * 128, (half + 1) * 128)
            whole = base[t, rows, :] + eighth[2 * t + half:2 * t + half + 1, :]
            gk_v[t, rows, :] = whole[:, :W].astype(BF)
            gv_v[t, rows, :] = whole[:, W:].astype(BF)
    for t in range(4):
        @pl.when(h != 1 + (t >> 1))
        def _():
            remote(outr.at[t], outr.at[t], ob_send.at[0, 0], ob_recv.at[t], pos, h).wait_recv()
    part_b.finish()

    for copy in d3:
        copy.wait_send()
    part_a.wait_back()
    part_b.wait_back()
    for tile in range(2):
        for c in range(4):
            @pl.when(jnp.logical_and(middle, h != c))
            def _():
                send_output(tile, c).wait_send()


def hand_over(*arrays):
    n = len(arrays)

    def copy_kernel(*refs):
        sems = refs[2 * n]
        copies = [pltpu.make_async_copy(refs[k], refs[n + k], sems.at[k]) for k in range(n)]
        for copy in copies:
            copy.start()
        for copy in copies:
            copy.wait()

    return pl.pallas_call(
        copy_kernel,
        out_shape=[jax.ShapeDtypeStruct(a.shape, a.dtype) for a in arrays],
        in_specs=[pl.BlockSpec(memory_space=pltpu.VMEM)] * n,
        out_specs=[pl.BlockSpec(memory_space=pltpu.HBM)] * n,
        scratch_shapes=[pltpu.SemaphoreType.DMA((n,))],
    )(*[pltpu.with_memory_space_constraint(a, pltpu.VMEM) for a in arrays])


def local(queries, keys, values, out_weight, cotangent):
    tiles = (4, TILE, W)

    def v(*shape, dtype=BF):
        return pltpu.VMEM(shape, dtype)

    def f(*shape):
        return pltpu.VMEM(shape, F32)

    dma = pltpu.SemaphoreType.DMA
    scratch = [
        v(4, 256, 256), v(4, 768, 256), v(4, 768, 256), v(4, 256, 768), v(4, 256, 768),
        v(1024, 1024), v(1024, 1024), f(2, 768, 256), v(4, 768, 1024), v(768, 1024),
        v(256, 1024), f(4, 256, 256), v(4, 256, 256), v(2, 256, 1024),
        v(2, 4, 256, 256),
        v(1024, 256), v(1024, 256), f(4, 8, 256), f(4, 256, 512),
        f(4, 64, 512), f(4, 64, 512), f(384, 512), f(4, 256, 256),
        v(8, 32, 768), v(8, 32, 768), v(4, 16, 384), v(8, 16, 384), v(4, 16, 384), v(8, 4, 16, 384),
        v(8, 32, 256), v(8, 32, 256), v(32, 256), v(8, 32, 256), v(32, 256), v(8, 32, 256),
        v(144, 256), v(80, 256), v(48, 256), v(144, 256), v(2, 80, 256), v(4, 48, 256),
        f(64, 512), v(128, 256), v(64, 256), v(32, 256),
        v(128, 256), v(2, 64, 256), v(4, 32, 256), v(384, 256), v(384, 256),
        v(128, 256), v(2, 64, 256), v(4, 32, 256), v(128, 256), v(2, 64, 256), v(4, 32, 256),
        v(128, 256), v(2, 64, 256), v(4, 32, 256), v(128, 256), v(2, 64, 256), v(4, 32, 256),
        v(8, 16, 256), v(8, 16, 256),
        dma((14,)), dma((2, 3, 4)), dma((2, 3, 4)),
        dma((7,)), dma((7,)), dma((7,)), dma((7,)),
        dma((4,)), dma((2, 4)), dma((2, 4)), dma((4,)),
    ] + [dma((2, 7))] * 8 + [dma((7,))] * 6
    out_shape = [pltpu.VMEM(tiles, BF)] * 4 + [pltpu.VMEM((256, 1024), F32)]
    output, gq, gk, gv, wg = pl.pallas_call(
        kernel,
        out_shape=out_shape,
        in_specs=[pl.BlockSpec(memory_space=pltpu.HBM)] * 5,
        out_specs=[pl.BlockSpec(memory_space=pltpu.VMEM)] * 5,
        scratch_shapes=scratch,
        compiler_params=pltpu.CompilerParams(
            collective_id=0, has_side_effects=True, vmem_limit_bytes=48 * 1024 * 1024
        ),
    )(*[
        pltpu.with_memory_space_constraint(a, pltpu.HBM)
        for a in (
            queries.reshape(tiles), keys.reshape(tiles), values.reshape(tiles), out_weight,
            cotangent.reshape(tiles),
        )
    ])
    output, gq, gk, gv, wg = hand_over(output, gq, gk, gv, wg)
    rows = queries.shape
    return output.reshape(rows), gq.reshape(rows), gk.reshape(rows), gv.reshape(rows), wg


def solution(mesh):
    in_specs = (P("tile", "head"), P("tile", "head"), P("tile", "head"), P(), P("tile", "head"))
    out_specs = (
        P("tile", "head"),
        P("tile", "head"),
        P("tile", "head"),
        P("tile", "head"),
        P("head", None),
    )
    return jax.shard_map(local, mesh=mesh, in_specs=in_specs, out_specs=out_specs, check_vma=False)
```
